32 devices in a mesh: tm: 8 (over z, y), mel: 4 (over x, core).
Axes of the slice: x: 2, y: 2, z: 4, core: 2. Of those that a mesh axis runs over, the one named last changes fastest.
Arguments:
- act_one: bfloat16 [1024, 16384], P('tm', 'mel'), may hold values from -6 to 6
- act_two: bfloat16 [1024, 16384], P('tm', 'mel'), may hold values from -6 to 6
- act_three: bfloat16 [512, 16384], P('tm', 'mel'), may hold values from -6 to 6
- act_four: bfloat16 [512, 16384], P('tm', 'mel'), may hold values from -6 to 6
- target_one: bfloat16 [512, 8192], P('tm', 'mel'), may hold values from -6 to 6
- target_two: bfloat16 [256, 8192], P('tm', 'mel'), may hold values from -6 to 6
- kernel_one: bfloat16 [3, 3, 1, 64], replicated, may hold values from -2 to 2
- kernel_two: bfloat16 [3, 3, 64, 64], replicated, may hold values from -0.25 to 0.25
- kernel_three: bfloat16 [3, 3, 64, 128], replicated, may hold values from -0.25 to 0.25
- kernel_four: bfloat16 [3, 3, 128, 128], replicated, may hold values from -0.1875 to 0.1875
- mel_power: float32 [1024, 256], P('tm', 'mel'), may hold values from 0.05 to 20
- loudness: float32 [256], P('mel'), may hold values from 0.1 to 10
- filters: float32 [512, 256], replicated, may hold values from -0.375 to 0.375
- spec_real: float32 [1024, 512], P('tm', 'mel'), may hold values from -6 to 6
- spec_imag: float32 [1024, 512], P('tm', 'mel'), may hold values from -6 to 6
Outputs:
- wave_grad: float32 [524288], P(('tm', 'mel'))
The draws below stay inside these ranges and needn't reach their ends.
All inputs are finite; a program needn't handle non-finite values.
Results may differ from the reference program's by a relative error of at most 0.015.
Values may be sent and summed in bfloat16 or wider, within the bound.
A program may use at most 64 MiB of HBM per device.

```python
import math
import jax
import jax.numpy as jnp
from jax import lax

MELS = 256
C1 = 64
C2 = 128
NFFT = 1024
BINS = 512
HOP = 512
FRAMES = 1024
SAMPLES = 524288


def steps_of(stream_key, dims, pieces, low, top_value):
    def one(axis_at, shards_of):
        steps = jax.random.uniform(jax.random.fold_in(jax.random.fold_in(stream_key, 6), axis_at), (shards_of,), jnp.float32, low / len(pieces), top_value / len(pieces))
        return jnp.repeat(jnp.exp(steps), dims[axis_at] // shards_of).reshape((-1,) + (1,) * (len(dims) - axis_at - 1))

    level = one(*pieces[0])
    for cut in pieces[1:]:
        level = level * one(*cut)
    return level


def noise(key, shape, deviation, reach, cuts=(), kind=jnp.bfloat16):
    level = steps_of(key, shape, cuts, -0.22, 0.18) if cuts else 1.0
    values = jax.random.normal(key, shape, jnp.float32) * deviation * level
    return jnp.minimum(jnp.maximum(values, -reach), reach).astype(kind)


def setup_inputs(seed: int = 0) -> dict:
    key_of = jax.random.split(jax.random.key(seed), 16)
    return {
        "act_one": noise(key_of[0], (FRAMES, MELS * C1), 1.0, 6.0, ((0, 8), (1, 4))),
        "act_two": noise(key_of[1], (FRAMES, MELS * C1), 1.0, 6.0, ((0, 8), (1, 4))),
        "act_three": noise(key_of[2], (FRAMES // 2, MELS // 2 * C2), 1.0, 6.0, ((0, 8), (1, 4))),
        "act_four": noise(key_of[3], (FRAMES // 2, MELS // 2 * C2), 1.0, 6.0, ((0, 8), (1, 4))),
        "target_one": noise(key_of[4], (FRAMES // 2, MELS // 2 * C1), 1.0, 6.0, ((0, 8), (1, 4))),
        "target_two": noise(key_of[5], (FRAMES // 4, MELS // 4 * C2), 1.0, 6.0, ((0, 8), (1, 4))),
        "kernel_one": noise(key_of[6], (3, 3, 1, C1), 9 ** -0.5, 2.0),
        "kernel_two": noise(key_of[7], (3, 3, C1, C1), (9 * C1) ** -0.5, 0.25),
        "kernel_three": noise(key_of[8], (3, 3, C1, C2), (9 * C1) ** -0.5, 0.25),
        "kernel_four": noise(key_of[9], (3, 3, C2, C2), (9 * C2) ** -0.5, 0.1875),
        "mel_power": jnp.clip(jnp.exp(math.log(20.0) - 5.9914645 * jax.random.uniform(key_of[10], (FRAMES, MELS), jnp.float32) ** steps_of(key_of[10], (FRAMES, MELS), ((0, 8), (1, 4)), -0.2, 0.2)), 0.05, 20.0),
        "loudness": jnp.clip(jnp.exp(math.log(10.0) - 4.6051702 * jax.random.uniform(key_of[11], (MELS,), jnp.float32) ** steps_of(key_of[11], (MELS,), ((0, 4),), -0.2, 0.2)), 0.1, 10.0),
        "filters": noise(key_of[12], (BINS, MELS), MELS ** -0.5, 0.375, (), jnp.float32),
        "spec_real": noise(key_of[13], (FRAMES, BINS), 1.0, 6.0, ((0, 8), (1, 4)), jnp.float32),
        "spec_imag": noise(key_of[14], (FRAMES, BINS), 1.0, 6.0, ((0, 8), (1, 4)), jnp.float32),
    }


def pool(values):
    rows, cols, chans = values.shape
    return 0.25 * jnp.sum(values.reshape(rows // 2, 2, cols // 2, 2, chans), axis=(1, 3))


def spread(grad):
    rows, cols, chans = grad.shape
    wide = jnp.broadcast_to(grad[:, None, :, None, :], (rows, 2, cols, 2, chans))
    return 0.25 * wide.reshape(rows * 2, cols * 2, chans)


def back_conv(grad, weights):
    kernel = jnp.transpose(weights[::-1, ::-1], (0, 1, 3, 2)).astype(jnp.float32)
    return lax.conv_general_dilated(grad.astype(jnp.float32)[None], kernel, (1, 1), ((1, 1), (1, 1)), dimension_numbers=("NHWC", "HWIO", "NHWC"), precision=lax.Precision.HIGHEST)[0]


def dft_table(offset, count):
    freqs = offset + jnp.arange(count, dtype=jnp.int32)
    points = jnp.arange(NFFT, dtype=jnp.int32)
    phase = (freqs[:, None] * points[None, :]) % NFFT
    angle = phase.astype(jnp.float32) * (2.0 * jnp.pi / NFFT)
    return jnp.concatenate([jnp.cos(angle), -jnp.sin(angle)], axis=0)


def reference(act_one, act_two, act_three, act_four, target_one, target_two, kernel_one, kernel_two, kernel_three, kernel_four, mel_power, loudness, filters, spec_real, spec_imag):
    first = act_one.reshape(FRAMES, MELS, C1)
    second = act_two.reshape(FRAMES, MELS, C1)
    third = act_three.reshape(FRAMES // 2, MELS // 2, C2)
    fourth = act_four.reshape(FRAMES // 2, MELS // 2, C2)
    feat_low = pool(jnp.maximum(second.astype(jnp.float32), 0.0))
    feat_high = pool(jnp.maximum(fourth.astype(jnp.float32), 0.0))
    diff_high = feat_high - target_two.reshape(FRAMES // 4, MELS // 4, C2).astype(jnp.float32)
    grad_four = jnp.where(fourth > 0, spread(diff_high), 0.0).astype(jnp.bfloat16)
    grad_three = jnp.where(third > 0, back_conv(grad_four, kernel_four), 0.0).astype(jnp.bfloat16)
    grad_pool = back_conv(grad_three, kernel_three) + feat_low - target_one.reshape(FRAMES // 2, MELS // 2, C1).astype(jnp.float32)
    grad_two = jnp.where(second > 0, spread(grad_pool), 0.0).astype(jnp.bfloat16)
    grad_one = jnp.where(first > 0, back_conv(grad_two, kernel_two), 0.0).astype(jnp.bfloat16)
    grad_log = back_conv(grad_one, kernel_one)[:, :, 0]
    grad_mel = grad_log * loudness[None, :] / (1.0 + loudness[None, :] * mel_power)
    grad_power = lax.dot_general(grad_mel, filters, (((1,), (1,)), ((), ())), precision=lax.Precision.HIGHEST)
    grad_re = 2.0 * grad_power * spec_real
    grad_im = 2.0 * grad_power * spec_imag
    points = jnp.arange(NFFT, dtype=jnp.int32).astype(jnp.float32)
    window = 0.5 - 0.5 * jnp.cos(points * (2.0 * jnp.pi / NFFT))
    frames = jnp.dot(jnp.concatenate([grad_re, grad_im], axis=1), dft_table(0, BINS), precision=lax.Precision.HIGHEST)
    frames = frames * window[None, :] * (NFFT ** -0.5)
    shifted = jnp.concatenate([jnp.zeros((1, HOP), jnp.float32), frames[:-1, HOP:]], axis=0)
    return (frames[:, :HOP] + shifted).reshape(SAMPLES)
```

```python
import functools

import jax
import jax.numpy as jnp
import ml_dtypes
import numpy as np
from jax import lax
from jax.experimental import pallas as pl
from jax.experimental.pallas import tpu as pltpu
from jax.sharding import PartitionSpec as P

LANES = 128
TILE = 16
SIDE = 4
EDGE = SIDE * LANES
MESH = pl.DeviceIdType.MESH
BF16 = jnp.bfloat16
F32 = jnp.float32

DEPTH = (1, 2, 2, 4, 1, 2)
PLACE = (0, 1, 3, 5, 9, 10)
WIDTH = (128, 128, 256, 512, 128, 256)


def synthesis_table(bins):
    points = 2 * bins
    sample = np.arange(points)
    angle = (np.arange(bins)[:, None] * sample[None, :] % points) * (2.0 * np.pi / points)
    window = 0.5 - 0.5 * np.cos(sample * (2.0 * np.pi / points))
    scale = 2.0 * window * points**-0.5
    table = np.concatenate([np.cos(angle) * scale, -np.sin(angle) * scale], axis=0)
    return table.astype(np.float32).astype(ml_dtypes.bfloat16)


def iota2(rows, cols):
    return (
        lax.broadcasted_iota(jnp.int32, (rows, cols), 0),
        lax.broadcasted_iota(jnp.int32, (rows, cols), 1),
    )


def as_bf16(mask, value=1.0):
    return jnp.where(mask, value, 0.0).astype(F32).astype(BF16)


def coarser(row, main):
    return row // 2 + jnp.where(row >= main + TILE // 2, TILE // 2, 0)


def dot(a, b):
    return jnp.dot(a, b, preferred_element_type=F32)


def dot_nt(a, b):
    return lax.dot_general(a, b, (((1,), (1,)), ((), ())), preferred_element_type=F32)


def kernel(
    n_tm,
    n_mel,
    act_one,
    act_two,
    act_three,
    act_four,
    target_one,
    target_two,
    filters,
    table,
    kernel_one,
    kernel_two,
    kernel_three,
    kernel_four,
    mel_power,
    loudness,
    spec_real,
    spec_imag,
    out,
    e1,
    e2,
    e3,
    e4,
    t1,
    t2,
    filters_v,
    table_v,
    pack,
    rows_in,
    ga,
    gb,
    gc,
    gd,
    w4,
    w3,
    w2,
    wb,
    spec_out,
    spec_in,
    mel_out,
    mel_in,
    load_sem,
    halo_send,
    halo_recv,
    spec_send,
    spec_recv,
    mel_send,
    mel_recv,
):
    tm, mel = lax.axis_index("tm"), lax.axis_index("mel")
    length = act_one.shape[1]
    inputs = (act_one, act_two, act_three, act_four, target_one, target_two)
    wide = (e1, e2, e3, e4, t1, t2)
    frames, coarse = act_one.shape[0], act_three.shape[0]
    fine_rows, coarse_rows = e1.shape[0], e3.shape[0]
    tiles = e1.shape[1] // LANES
    share = frames // n_mel

    loads = []
    for at, (src, dst) in enumerate(zip(inputs, wide)):
        rows, cols = src.shape
        loads.append(
            pltpu.make_async_copy(
                src, dst.at[pl.ds(0, rows), pl.ds(EDGE, cols)], load_sem.at[at]
            )
        )
    loads.append(pltpu.make_async_copy(filters, filters_v, load_sem.at[6]))
    loads.append(pltpu.make_async_copy(table, table_v, load_sem.at[7]))
    for load in loads:
        load.start()

    for src, dst in zip(inputs, wide):
        rows, cols = src.shape
        dst[pl.ds(0, rows), pl.ds(0, EDGE)] = jnp.zeros((rows, EDGE), BF16)
        dst[pl.ds(0, rows), pl.ds(EDGE + cols, EDGE)] = jnp.zeros((rows, EDGE), BF16)
    rows_in[...] = jnp.zeros(rows_in.shape, BF16)
    spec_in[...] = jnp.zeros(spec_in.shape, BF16)
    mel_in[...] = jnp.zeros(mel_in.shape, BF16)

    barrier = pltpu.get_barrier_semaphore()

    def has(dt, dm):
        cond = jnp.bool_(True)
        if dt:
            cond = (tm > 0) if dt < 0 else (tm < n_tm - 1)
        if dm:
            side = (mel > 0) if dm < 0 else (mel < n_mel - 1)
            cond = side if not dt else jnp.logical_and(cond, side)
        return cond

    for dt in (-1, 0, 1):
        for k in range(n_mel):
            if dt == 0 and k == 0:
                continue

            def greet(dt=dt, k=k):
                pl.semaphore_signal(
                    barrier,
                    inc=1,
                    device_id={"tm": tm + dt, "mel": lax.rem(mel + k, n_mel)},
                    device_id_type=MESH,
                )

            if dt:
                pl.when(has(dt, 0))(greet)
            else:
                greet()
    rows_of_peers = 1 + jnp.where(tm > 0, 1, 0) + jnp.where(tm < n_tm - 1, 1, 0)
    pl.semaphore_wait(barrier, n_mel * rows_of_peers - 1)

    halo = []

    def add_halo(dt, dm, src, dst):
        at = len(halo)
        copy = pltpu.make_async_remote_copy(
            src_ref=src,
            dst_ref=dst,
            send_sem=halo_send.at[at],
            recv_sem=halo_recv.at[at],
            device_id={"tm": tm + dt, "mel": mel + dm},
            device_id_type=MESH,
        )
        halo.append((dt, dm, copy))
        pl.when(has(dt, dm))(copy.start)

    for src, dst, width in zip(inputs, wide, WIDTH):
        rows, cols = src.shape
        add_halo(
            0,
            1,
            src.at[:, pl.ds(cols - width, width)],
            dst.at[pl.ds(0, rows), pl.ds(EDGE - width, width)],
        )
        add_halo(
            0,
            -1,
            src.at[:, pl.ds(0, width)],
            dst.at[pl.ds(0, rows), pl.ds(EDGE + cols, width)],
        )

    def exchange(src, dst, send, recv):
        copies = []
        for k in range(n_mel):
            j = lax.rem(mel + k, n_mel)
            main = pl.ds(pl.multiple_of(j * share, TILE), share)
            before = pl.ds(
                pl.multiple_of(lax.rem(j * share + frames - TILE, frames), TILE), TILE
            )
            if k:
                copy = pltpu.make_async_remote_copy(
                    src_ref=src.at[main],
                    dst_ref=dst.at[mel, pl.ds(0, share)],
                    send_sem=send.at[k],
                    recv_sem=recv.at[k],
                    device_id={"tm": tm, "mel": j},
                    device_id_type=MESH,
                )
                copy.start()
                copies.append((copy, None, None))
            copy = pltpu.make_async_remote_copy(
                src_ref=src.at[before],
                dst_ref=dst.at[mel, pl.ds(share, TILE)],
                send_sem=send.at[n_mel + k],
                recv_sem=recv.at[n_mel + k],
                device_id={"tm": tm + jnp.where(j == 0, 1, 0), "mel": j},
                device_id_type=MESH,
            )
            if k:
                sends = jnp.logical_or(j > 0, tm < n_tm - 1)
                receives = jnp.logical_or(mel > 0, tm > 0)
            else:
                sends = jnp.logical_and(mel == 0, tm < n_tm - 1)
                receives = jnp.logical_and(mel == 0, tm > 0)
            pl.when(sends)(copy.start)
            copies.append((copy, sends, receives))
        dst[mel, pl.ds(0, share)] = src[pl.ds(pl.multiple_of(mel * share, TILE), share)]

        @pl.when(mel > 0)
        def _():
            dst[mel, pl.ds(share, TILE)] = src[
                pl.ds(pl.multiple_of(mel * share - TILE, TILE), TILE)
            ]

        return copies

    def finish(copies):
        for copy, sends, receives in copies:
            if sends is None:
                copy.wait_recv()
            else:
                pl.when(receives)(copy.wait_recv)
        for copy, sends, receives in copies:
            if sends is None:
                copy.wait_send()
            else:
                pl.when(sends)(copy.wait_send)

    spec_out[:, pl.ds(0, spec_real.shape[1])] = spec_real[...].astype(BF16)
    spec_out[:, pl.ds(spec_real.shape[1], spec_imag.shape[1])] = spec_imag[...].astype(BF16)

    for load in loads[:6]:
        load.wait()
    o, c = iota2(TILE, 6 * TILE)
    first_rows = jnp.zeros((TILE, 6 * TILE), jnp.bool_)
    last_rows = jnp.zeros((TILE, 6 * TILE), jnp.bool_)
    for x in range(6):
        inside = (o >= PLACE[x]) & (o < PLACE[x] + DEPTH[x])
        first_rows |= inside & (c - x * TILE == o - PLACE[x])
        last_rows |= inside & (c - x * TILE - (TILE - DEPTH[x]) == o - PLACE[x])
    picks = (as_bf16(first_rows), as_bf16(last_rows))
    target_length = target_one.shape[1]
    for chunk in range(length // EDGE):
        for end in (0, 1):
            parts = []
            for x, (src, dst) in enumerate(zip(inputs, wide)):
                lane = EDGE + (chunk * EDGE) % (target_length if x >= 4 else length)
                row = src.shape[0] - TILE if end else 0
                parts.append(dst[pl.ds(row, TILE), pl.ds(lane, EDGE)])
            pack[end, :, pl.ds(chunk * EDGE, EDGE)] = dot(
                picks[end], jnp.concatenate(parts, axis=0)
            ).astype(BF16)
    for end, dt in ((1, 1), (0, -1)):
        at = 1 - end
        add_halo(dt, 0, pack.at[end], rows_in.at[at, :, pl.ds(EDGE, length)])
        add_halo(
            dt, 1, pack.at[end, :, pl.ds(length - EDGE, EDGE)], rows_in.at[at, :, pl.ds(0, EDGE)]
        )
        add_halo(
            dt, -1, pack.at[end, :, pl.ds(0, EDGE)], rows_in.at[at, :, pl.ds(EDGE + length, EDGE)]
        )
    spec_copies = exchange(spec_out, spec_in, spec_send, spec_recv)

    w4[...] = jnp.zeros(w4.shape, BF16)
    w3[...] = jnp.zeros(w3.shape, BF16)
    half = LANES // 2
    blank = jnp.zeros((half, half), F32)
    for i in range(3):
        for k in range(4):
            lanes = pl.ds((i * 4 + k) * LANES, LANES)
            for n in range(2):
                j = n - (k - 1)
                if abs(j) <= 1:
                    w4[pl.ds(n * LANES, LANES), lanes] = kernel_four[i, j + 1]
                    w3[pl.ds(n * LANES, half), lanes] = kernel_three[i, j + 1]
                    w3[pl.ds(n * LANES + half, half), lanes] = kernel_three[i, j + 1]
                for a in range(2):
                    pair = []
                    for b in range(2):
                        j = (2 * n + a) - (2 * (k - 1) + b)
                        pair.append(
                            kernel_two[i, j + 1].astype(F32) if abs(j) <= 1 else blank
                        )
                    w2[pl.ds(n * LANES + a * half, half), lanes] = jnp.concatenate(
                        pair, axis=1
                    ).astype(BF16)
    mels = mel_power.shape[1]
    one = kernel_one[...].astype(F32)
    one = jnp.concatenate([one, one], axis=1)
    m, lane = iota2(mels, LANES)

    def band(s, carry):
        d = m - (2 * (s - SIDE) + lane // half)
        for i in range(3):
            value = jnp.zeros((mels, LANES), F32)
            for j in range(3):
                value = jnp.where(d == j - 1, one[3 * i + j][None, :], value)
            wb[s, pl.ds(i * mels, mels)] = value.astype(BF16)
        wb[s, pl.ds(3 * mels, mels)] = jnp.zeros((mels, LANES), BF16)
        return carry

    lax.fori_loop(2, tiles - 2, band, 0)
    for g in (gb, gc):
        for s in (1, tiles - 2):
            for i in range(3):
                g[i, s] = jnp.zeros(g.shape[2:], BF16)

    for dt, dm, copy in halo:
        pl.when(has(-dt, -dm))(copy.wait_recv)
    o, c = iota2(6 * TILE, 2 * TILE)
    spots = jnp.zeros((6 * TILE, 2 * TILE), jnp.bool_)
    for x in range(6):
        for at, base in ((0, TILE - DEPTH[x]), (1, 0)):
            r, p = o - x * TILE - base, c - at * TILE - PLACE[x]
            spots |= (r == p) & (r >= 0) & (r < DEPTH[x])
    spots = as_bf16(spots)
    chunks = (length + 2 * EDGE) // EDGE
    target_chunks = target_length // EDGE
    for chunk in range(chunks):
        lanes = pl.ds(chunk * EDGE, EDGE)
        both = jnp.concatenate([rows_in[0, :, lanes], rows_in[1, :, lanes]], axis=0)
        placed = dot(spots, both).astype(BF16)
        for x, (src, dst) in enumerate(zip(inputs, wide)):
            at = lanes
            if x >= 4:
                if chunk == chunks - 1:
                    at = pl.ds((target_chunks + 1) * EDGE, EDGE)
                elif chunk > target_chunks:
                    continue
            dst[pl.ds(src.shape[0], TILE), at] = placed[x * TILE : (x + 1) * TILE]

    def shifted(g, s, value):
        rows = value.shape[0]
        g[0, s] = pltpu.roll(value, rows - 1, 0).astype(BF16)
        g[1, s] = value.astype(BF16)
        g[2, s] = pltpu.roll(value, 1, 0).astype(BF16)

    def tile_at(s, count=1):
        return pl.ds(pl.multiple_of(s * LANES, LANES), count * LANES)

    r, s_ = iota2(coarse_rows, coarse_rows)
    mean_rows = as_bf16(r // 2 == s_ // 2, 0.25)
    r, s_ = iota2(coarse_rows, t2.shape[0])
    spread_two = as_bf16(coarser(r, coarse) == s_)

    def top(p, carry):
        x = e4[:, tile_at(2 * p, 2)].astype(F32)
        means = dot(mean_rows, jnp.maximum(x, 0.0).astype(BF16))
        wanted = dot(spread_two, t2[:, tile_at(p + SIDE // 2)])
        diff = 0.25 * (means[:, :LANES] + means[:, LANES:] - wanted)
        for n in range(2):
            shifted(ga, 2 * p + n, jnp.where(x[:, n * LANES : (n + 1) * LANES] > 0, diff, 0.0))
        return carry

    lax.fori_loop(0, tiles // 2, top, 0)

    def conv(g, weights, group, epilogue):
        rows = g.shape[2]
        pairs = (tiles - 4) // 2

        def step(q, carry):
            base = 2 + 2 * group * q
            lhs = jnp.concatenate(
                [
                    jnp.concatenate(
                        [g[i, base + 2 * u - 1 + k] for i in range(3) for k in range(4)], axis=1
                    )
                    for u in range(group)
                ],
                axis=0,
            )
            result = dot_nt(lhs, weights[...])
            for u in range(group):
                epilogue(base + 2 * u, result[u * rows : (u + 1) * rows])
            return carry

        lax.fori_loop(0, pairs // group, step, 0)

    def third(s, value):
        x = e3[:, tile_at(s, 2)].astype(F32)
        masked = jnp.where(x > 0, value, 0.0)
        for n in range(2):
            shifted(gb, s + n, masked[:, n * LANES : (n + 1) * LANES])

    conv(ga, w4, 6, third)

    r, s_ = iota2(coarse_rows, fine_rows)
    pool_rows = as_bf16(coarser(s_, frames) == r, 0.25)
    r, s_ = iota2(fine_rows, coarse_rows)
    spread_rows = as_bf16(coarser(r, frames) == s_)
    low = lax.broadcasted_iota(jnp.int32, (coarse_rows, LANES), 1) < half

    def second(s, value):
        x = e2[:, tile_at(s, 2)].astype(F32)
        sums = dot(pool_rows, jnp.maximum(x, 0.0).astype(BF16))
        want = t1[:, tile_at((s - SIDE) // 2 + SIDE)].astype(F32)
        turned = pltpu.roll(want, half, 1)
        wants = (jnp.where(low, want, turned), jnp.where(low, turned, want))
        parts = []
        for n in range(2):
            lanes = slice(n * LANES, (n + 1) * LANES)
            feat = sums[:, lanes] + pltpu.roll(sums[:, lanes], half, 1)
            parts.append((0.25 * (value[:, lanes] + feat - wants[n])).astype(BF16))
        fine = dot(spread_rows, jnp.concatenate(parts, axis=1))
        masked = jnp.where(x > 0, fine, 0.0)
        for n in range(2):
            shifted(gc, s + n, masked[:, n * LANES : (n + 1) * LANES])

    conv(gb, w3, 6, second)

    def first(s, value):
        x = e1[:, tile_at(s, 2)].astype(F32)
        masked = jnp.where(x > 0, value, 0.0).astype(BF16)
        for n in range(2):
            gd[s + n] = masked[:, n * LANES : (n + 1) * LANES]

    conv(gc, w2, 3, first)

    total = jnp.zeros((fine_rows, 4 * mels), F32)
    for s in range(2, tiles - 2, 2):
        total += dot_nt(
            jnp.concatenate([gd[s], gd[s + 1]], axis=1),
            jnp.concatenate([wb[s], wb[s + 1]], axis=1),
        )
    left, right = total[:, : 2 * mels], total[:, 2 * mels :]
    grad_log = (
        pltpu.roll(left, fine_rows - 1, 0) + pltpu.roll(left, mels, 1) + pltpu.roll(right, 1, 0)
    )[:frames, :mels]
    loud = loudness[...]
    grad_mel = grad_log * loud / (1.0 + loud * mel_power[...])
    twice = jnp.concatenate([grad_mel, grad_mel], axis=1)
    lane = lax.broadcasted_iota(jnp.int32, twice.shape, 1)
    mel_out[...] = jnp.where(lane // mels == lax.rem(mel, 2), twice, 0.0).astype(BF16)
    mel_copies = exchange(mel_out, mel_in, mel_send, mel_recv)

    for dt, dm, copy in halo:
        pl.when(has(dt, dm))(copy.wait_send)
    finish(spec_copies)
    loads[6].wait()
    loads[7].wait()
    finish(mel_copies)

    whole = jnp.concatenate(
        [mel_in[2 * a] + mel_in[2 * a + 1] for a in range(n_mel // 2)], axis=1
    )
    power = dot_nt(whole, filters_v[...].astype(BF16))
    per = spec_real.shape[1]
    grads = []
    for part in range(2):
        for j in range(n_mel):
            spec = spec_in[j, :, pl.ds(part * per, per)].astype(F32)
            grads.append((power[:, j * per : (j + 1) * per] * spec).astype(BF16))
    made = dot(jnp.concatenate(grads, axis=1), table_v[...])
    hop = made.shape[1] // 2
    blocks = made[:, :hop] + pltpu.roll(made[:, hop:], 1, 0)
    for a in range(hop // LANES):
        out[pl.ds(a, share, stride=hop // LANES), :] = blocks[
            :share, a * LANES : (a + 1) * LANES
        ]


def shards(
    act_one,
    act_two,
    act_three,
    act_four,
    target_one,
    target_two,
    kernel_one,
    kernel_two,
    kernel_three,
    kernel_four,
    mel_power,
    loudness,
    filters,
    spec_real,
    spec_imag,
):
    n_tm, n_mel = lax.axis_size("tm"), lax.axis_size("mel")
    frames, mels = mel_power.shape
    bins = filters.shape[0]
    table = jnp.asarray(synthesis_table(bins))
    share = frames // n_mel
    ext = lambda a: pltpu.VMEM((a.shape[0] + TILE, a.shape[1] + 2 * EDGE), BF16)
    length = act_one.shape[1]
    tiles = (length + 2 * EDGE) // LANES
    fine_rows, coarse_rows = frames + TILE, frames // 2 + TILE
    any_spec = pl.BlockSpec(memory_space=pl.ANY)
    vmem = pl.BlockSpec(memory_space=pltpu.VMEM)
    result = pl.pallas_call(
        functools.partial(kernel, n_tm, n_mel),
        out_shape=jax.ShapeDtypeStruct((share * bins // LANES, LANES), F32),
        in_specs=[any_spec] * 8 + [vmem] * 8,
        out_specs=vmem,
        scratch_shapes=[
            ext(act_one),
            ext(act_two),
            ext(act_three),
            ext(act_four),
            ext(target_one),
            ext(target_two),
            pltpu.VMEM(filters.shape, F32),
            pltpu.VMEM(table.shape, BF16),
            pltpu.VMEM((2, TILE, length), BF16),
            pltpu.VMEM((2, TILE, length + 2 * EDGE), BF16),
            pltpu.VMEM((3, tiles, coarse_rows, LANES), BF16),
            pltpu.VMEM((3, tiles, coarse_rows, LANES), BF16),
            pltpu.VMEM((3, tiles, fine_rows, LANES), BF16),
            pltpu.VMEM((tiles, fine_rows, LANES), BF16),
            pltpu.VMEM((2 * LANES, 12 * LANES), BF16),
            pltpu.VMEM((2 * LANES, 12 * LANES), BF16),
            pltpu.VMEM((2 * LANES, 12 * LANES), BF16),
            pltpu.VMEM((tiles, 4 * mels, LANES), BF16),
            pltpu.VMEM((frames, 2 * spec_real.shape[1]), BF16),
            pltpu.VMEM((n_mel, share + TILE, 2 * spec_real.shape[1]), BF16),
            pltpu.VMEM((frames, 2 * mels), BF16),
            pltpu.VMEM((n_mel, share + TILE, 2 * mels), BF16),
            pltpu.SemaphoreType.DMA((8,)),
            pltpu.SemaphoreType.DMA((18,)),
            pltpu.SemaphoreType.DMA((18,)),
            pltpu.SemaphoreType.DMA((2 * n_mel,)),
            pltpu.SemaphoreType.DMA((2 * n_mel,)),
            pltpu.SemaphoreType.DMA((2 * n_mel,)),
            pltpu.SemaphoreType.DMA((2 * n_mel,)),
        ],
        compiler_params=pltpu.CompilerParams(
            collective_id=0, has_side_effects=True, vmem_limit_bytes=56 * 2**20
        ),
        name="wave_gradient",
    )(
        act_one,
        act_two,
        act_three,
        act_four,
        target_one,
        target_two,
        filters,
        table,
        kernel_one.reshape(9, kernel_one.shape[3]),
        kernel_two,
        kernel_three,
        kernel_four,
        mel_power,
        loudness.reshape(1, mels),
        spec_real,
        spec_imag,
    )
    return result.reshape(-1)


def solution(mesh):
    return jax.shard_map(
        shards,
        mesh=mesh,
        in_specs=(
            P("tm", "mel"),
            P("tm", "mel"),
            P("tm", "mel"),
            P("tm", "mel"),
            P("tm", "mel"),
            P("tm", "mel"),
            P(),
            P(),
            P(),
            P(),
            P("tm", "mel"),
            P("mel"),
            P(),
            P("tm", "mel"),
            P("tm", "mel"),
        ),
        out_specs=P(("tm", "mel")),
        check_vma=False,
    )
```

```python
import functools

import jax
import jax.numpy as jnp
import ml_dtypes
import numpy as np
from jax import lax
from jax.experimental import pallas as pl
from jax.experimental.pallas import tpu as pltpu
from jax.sharding import PartitionSpec as P

LANES = 128
TILE = 16
SIDE = 4
EDGE = SIDE * LANES
MESH = pl.DeviceIdType.MESH
BF16 = jnp.bfloat16
F32 = jnp.float32

DEPTH = (1, 2, 2, 4, 1, 2)
PLACE = (0, 1, 3, 5, 9, 10)
WIDTH = (128, 128, 256, 512, 128, 256)


def synthesis_table(bins):
    points = 2 * bins
    sample = np.arange(points)
    angle = (np.arange(bins)[:, None] * sample[None, :] % points) * (2.0 * np.pi / points)
    window = 0.5 - 0.5 * np.cos(sample * (2.0 * np.pi / points))
    scale = 2.0 * window * points**-0.5
    table = np.concatenate([np.cos(angle) * scale, -np.sin(angle) * scale], axis=0)
    return table.astype(np.float32).astype(ml_dtypes.bfloat16)


def iota2(rows, cols):
    return (
        lax.broadcasted_iota(jnp.int32, (rows, cols), 0),
        lax.broadcasted_iota(jnp.int32, (rows, cols), 1),
    )


def as_bf16(mask, value=1.0):
    return jnp.where(mask, value, 0.0).astype(F32).astype(BF16)


def coarser(row, main):
    return row // 2 + jnp.where(row >= main + TILE // 2, TILE // 2, 0)


def dot(a, b):
    return jnp.dot(a, b, preferred_element_type=F32)


def dot_nt(a, b):
    return lax.dot_general(a, b, (((1,), (1,)), ((), ())), preferred_element_type=F32)


def kernel(
    n_tm,
    n_mel,
    act_one,
    act_two,
    act_three,
    act_four,
    target_one,
    target_two,
    filters,
    table,
    kernel_one,
    kernel_two,
    kernel_three,
    kernel_four,
    mel_power,
    loudness,
    spec_real,
    spec_imag,
    out,
    e1,
    e2,
    e3,
    e4,
    t1,
    t2,
    filters_v,
    table_v,
    pack,
    rows_in,
    ga,
    gb,
    gc,
    gd,
    pre,
    gain,
    filters_b,
    k2_v,
    k3_v,
    k4_v,
    power_v,
    real_v,
    imag_v,
    w4,
    w3,
    w2,
    wb,
    spec_out,
    spec_in,
    mel_out,
    mel_in,
    load_sem,
    halo_send,
    halo_recv,
    spec_send,
    spec_recv,
    mel_send,
    mel_recv,
):
    tm, mel = lax.axis_index("tm"), lax.axis_index("mel")
    length = act_one.shape[1]
    inputs = (act_one, act_two, act_three, act_four, target_one, target_two)
    wide = (e1, e2, e3, e4, t1, t2)
    frames, coarse = act_one.shape[0], act_three.shape[0]
    fine_rows, coarse_rows = e1.shape[0], e3.shape[0]
    tiles = e1.shape[1] // LANES
    share = frames // n_mel

    loads = []
    for at, (src, dst) in enumerate(zip(inputs, wide)):
        rows, cols = src.shape
        loads.append(
            pltpu.make_async_copy(
                src, dst.at[pl.ds(0, rows), pl.ds(EDGE, cols)], load_sem.at[at]
            )
        )
    for src, dst in (
        (kernel_two, k2_v),
        (kernel_three, k3_v),
        (kernel_four, k4_v),
        (mel_power, power_v),
        (spec_real, real_v),
        (spec_imag, imag_v),
        (filters, filters_v),
        (table, table_v),
    ):
        loads.append(pltpu.make_async_copy(src, dst, load_sem.at[len(loads)]))
    for load in loads:
        load.start()

    for src, dst in zip(inputs, wide):
        rows, cols = src.shape
        dst[pl.ds(0, rows), pl.ds(0, EDGE)] = jnp.zeros((rows, EDGE), BF16)
        dst[pl.ds(0, rows), pl.ds(EDGE + cols, EDGE)] = jnp.zeros((rows, EDGE), BF16)
    rows_in[...] = jnp.zeros(rows_in.shape, BF16)
    spec_in[...] = jnp.zeros(spec_in.shape, BF16)
    mel_in[...] = jnp.zeros(mel_in.shape, BF16)

    barrier = pltpu.get_barrier_semaphore()

    def has(dt, dm):
        cond = jnp.bool_(True)
        if dt:
            cond = (tm > 0) if dt < 0 else (tm < n_tm - 1)
        if dm:
            side = (mel > 0) if dm < 0 else (mel < n_mel - 1)
            cond = side if not dt else jnp.logical_and(cond, side)
        return cond

    for dt in (-1, 0, 1):
        for k in range(n_mel):
            if dt == 0 and k == 0:
                continue

            def greet(dt=dt, k=k):
                pl.semaphore_signal(
                    barrier,
                    inc=1,
                    device_id={"tm": tm + dt, "mel": lax.rem(mel + k, n_mel)},
                    device_id_type=MESH,
                )

            if dt:
                pl.when(has(dt, 0))(greet)
            else:
                greet()

    halo = []

    def add_halo(dt, dm, src, dst):
        at = len(halo)
        copy = pltpu.make_async_remote_copy(
            src_ref=src,
            dst_ref=dst,
            send_sem=halo_send.at[at],
            recv_sem=halo_recv.at[at],
            device_id={"tm": tm + dt, "mel": mel + dm},
            device_id_type=MESH,
        )
        halo.append((dt, dm, copy))
        pl.when(has(dt, dm))(copy.start)

    def exchange(src, dst, send, recv):
        copies = []
        for k in range(n_mel):
            j = lax.rem(mel + k, n_mel)
            main = pl.ds(pl.multiple_of(j * share, TILE), share)
            before = pl.ds(
                pl.multiple_of(lax.rem(j * share + frames - TILE, frames), TILE), TILE
            )
            if k:
                copy = pltpu.make_async_remote_copy(
                    src_ref=src.at[main],
                    dst_ref=dst.at[mel, pl.ds(0, share)],
                    send_sem=send.at[k],
                    recv_sem=recv.at[k],
                    device_id={"tm": tm, "mel": j},
                    device_id_type=MESH,
                )
                copy.start()
                copies.append((copy, None, None))
            copy = pltpu.make_async_remote_copy(
                src_ref=src.at[before],
                dst_ref=dst.at[mel, pl.ds(share, TILE)],
                send_sem=send.at[n_mel + k],
                recv_sem=recv.at[n_mel + k],
                device_id={"tm": tm + jnp.where(j == 0, 1, 0), "mel": j},
                device_id_type=MESH,
            )
            if k:
                sends = jnp.logical_or(j > 0, tm < n_tm - 1)
                receives = jnp.logical_or(mel > 0, tm > 0)
            else:
                sends = jnp.logical_and(mel == 0, tm < n_tm - 1)
                receives = jnp.logical_and(mel == 0, tm > 0)
            pl.when(sends)(copy.start)
            copies.append((copy, sends, receives))
        dst[mel, pl.ds(0, share)] = src[pl.ds(pl.multiple_of(mel * share, TILE), share)]

        @pl.when(mel > 0)
        def _():
            dst[mel, pl.ds(share, TILE)] = src[
                pl.ds(pl.multiple_of(mel * share - TILE, TILE), TILE)
            ]

        return copies

    def finish(copies):
        for copy, sends, receives in copies:
            if sends is None:
                copy.wait_recv()
            else:
                pl.when(receives)(copy.wait_recv)
        for copy, sends, receives in copies:
            if sends is None:
                copy.wait_send()
            else:
                pl.when(sends)(copy.wait_send)

    for load in loads[:6]:
        load.wait()
    o, c = iota2(TILE, 6 * TILE)
    first_rows = jnp.zeros((TILE, 6 * TILE), jnp.bool_)
    last_rows = jnp.zeros((TILE, 6 * TILE), jnp.bool_)
    for x in range(6):
        inside = (o >= PLACE[x]) & (o < PLACE[x] + DEPTH[x])
        first_rows |= inside & (c - x * TILE == o - PLACE[x])
        last_rows |= inside & (c - x * TILE - (TILE - DEPTH[x]) == o - PLACE[x])
    picks = (as_bf16(first_rows), as_bf16(last_rows))
    target_length = target_one.shape[1]
    for chunk in range(length // EDGE):
        for end in (0, 1):
            parts = []
            for x, (src, dst) in enumerate(zip(inputs, wide)):
                lane = EDGE + (chunk * EDGE) % (target_length if x >= 4 else length)
                row = src.shape[0] - TILE if end else 0
                parts.append(dst[pl.ds(row, TILE), pl.ds(lane, EDGE)])
            pack[end, :, pl.ds(chunk * EDGE, EDGE)] = dot(
                picks[end], jnp.concatenate(parts, axis=0)
            ).astype(BF16)
    for load in loads[10:12]:
        load.wait()
    per = spec_real.shape[1]
    spec_out[:, pl.ds(0, per)] = real_v[...].astype(BF16)
    spec_out[:, pl.ds(per, per)] = imag_v[...].astype(BF16)

    rows_of_peers = 1 + jnp.where(tm > 0, 1, 0) + jnp.where(tm < n_tm - 1, 1, 0)
    pl.semaphore_wait(barrier, n_mel * rows_of_peers - 1)
    for end, dt in ((1, 1), (0, -1)):
        at = 1 - end
        add_halo(dt, 0, pack.at[end], rows_in.at[at, :, pl.ds(EDGE, length)])
        add_halo(
            dt, 1, pack.at[end, :, pl.ds(length - EDGE, EDGE)], rows_in.at[at, :, pl.ds(0, EDGE)]
        )
        add_halo(
            dt, -1, pack.at[end, :, pl.ds(0, EDGE)], rows_in.at[at, :, pl.ds(EDGE + length, EDGE)]
        )
    for src, dst, width in zip(inputs, wide, WIDTH):
        rows, cols = src.shape
        add_halo(
            0,
            1,
            src.at[:, pl.ds(cols - width, width)],
            dst.at[pl.ds(0, rows), pl.ds(EDGE - width, width)],
        )
        add_halo(
            0,
            -1,
            src.at[:, pl.ds(0, width)],
            dst.at[pl.ds(0, rows), pl.ds(EDGE + cols, width)],
        )
    spec_copies = exchange(spec_out, spec_in, spec_send, spec_recv)

    for load in loads[6:10]:
        load.wait()
    w4[...] = jnp.zeros(w4.shape, BF16)
    w3[...] = jnp.zeros(w3.shape, BF16)
    half = LANES // 2
    blank = jnp.zeros((half, half), F32)
    for i in range(3):
        for k in range(4):
            lanes = pl.ds((i * 4 + k) * LANES, LANES)
            for n in range(2):
                j = n - (k - 1)
                if abs(j) <= 1:
                    w4[pl.ds(n * LANES, LANES), lanes] = k4_v[i, j + 1]
                    w3[pl.ds(n * LANES, half), lanes] = k3_v[i, j + 1]
                    w3[pl.ds(n * LANES + half, half), lanes] = k3_v[i, j + 1]
                for a in range(2):
                    pair = []
                    for b in range(2):
                        j = (2 * n + a) - (2 * (k - 1) + b)
                        pair.append(
                            k2_v[i, j + 1].astype(F32) if abs(j) <= 1 else blank
                        )
                    w2[pl.ds(n * LANES + a * half, half), lanes] = jnp.concatenate(
                        pair, axis=1
                    ).astype(BF16)
    mels = mel_power.shape[0]
    one = kernel_one[...].astype(F32)
    one = jnp.concatenate([one, one], axis=2)
    m, lane = iota2(mels, LANES)

    def band(s, carry):
        d = m - (2 * (s - SIDE) + lane // half)
        for i in range(3):
            value = jnp.zeros((mels, LANES), F32)
            for j in range(3):
                value = jnp.where(d == j - 1, one[i, j][None, :], value)
            wb[s, pl.ds(i * mels, mels)] = value.astype(BF16)
        wb[s, pl.ds(3 * mels, mels)] = jnp.zeros((mels, LANES), BF16)
        return carry

    lax.fori_loop(2, tiles - 2, band, 0)
    for g in (gb, gc):
        for s in (1, tiles - 2):
            for i in range(3):
                g[i, s] = jnp.zeros(g.shape[2:], BF16)

    loud = loudness[...]
    level = loud / (1.0 + loud * jnp.transpose(power_v[...]))
    level = jnp.concatenate([level, level], axis=1)
    lane = lax.broadcasted_iota(jnp.int32, level.shape, 1)
    gain[...] = jnp.where(lane // mels == lax.rem(mel, 2), level, 0.0)
    loads[12].wait()
    filters_b[...] = filters_v[...].astype(BF16)

    def tile_at(s, count=1):
        return pl.ds(pl.multiple_of(s * LANES, LANES), count * LANES)

    def prepare(s, pairs, fine_at, coarse_at, matrix):
        rows_at = pl.ds(coarse_at, matrix.shape[0])
        x = e2[pl.ds(fine_at, matrix.shape[1]), tile_at(s, 2 * pairs)]
        sums = dot(matrix, jnp.maximum(x, jnp.zeros_like(x)))
        low = lax.broadcasted_iota(jnp.int32, (matrix.shape[0], LANES), 1) < half
        for u in range(pairs):
            want = t1[rows_at, tile_at((s - SIDE) // 2 + SIDE + u)].astype(F32)
            turned = pltpu.roll(want, half, 1)
            wants = (jnp.where(low, want, turned), jnp.where(low, turned, want))
            for n in range(2):
                at = 2 * u + n
                block = sums[:, at * LANES : (at + 1) * LANES]
                pre[s + at, rows_at] = 0.25 * (block + pltpu.roll(block, half, 1) - wants[n])

    r, s_ = iota2(coarse, frames)
    pool_main = as_bf16(s_ // 2 == r, 0.25)
    r, s_ = iota2(TILE, TILE)
    pool_tail = as_bf16(coarser(s_, 0) == r, 0.25)

    def early(q, carry):
        prepare(SIDE + 8 * q, 4, 0, 0, pool_main)
        return carry

    lax.fori_loop(0, (tiles - 2 * SIDE) // 8, early, 0)

    for dt, dm, copy in halo:
        pl.when(has(-dt, -dm))(copy.wait_recv)
    o, c = iota2(6 * TILE, 2 * TILE)
    spots = jnp.zeros((6 * TILE, 2 * TILE), jnp.bool_)
    for x in range(6):
        for at, base in ((0, TILE - DEPTH[x]), (1, 0)):
            r, p = o - x * TILE - base, c - at * TILE - PLACE[x]
            spots |= (r == p) & (r >= 0) & (r < DEPTH[x])
    spots = as_bf16(spots)
    chunks = (length + 2 * EDGE) // EDGE
    target_chunks = target_length // EDGE
    for chunk in range(chunks):
        lanes = pl.ds(chunk * EDGE, EDGE)
        both = jnp.concatenate([rows_in[0, :, lanes], rows_in[1, :, lanes]], axis=0)
        placed = dot(spots, both).astype(BF16)
        for x, (src, dst) in enumerate(zip(inputs, wide)):
            at = lanes
            if x >= 4:
                if chunk == chunks - 1:
                    at = pl.ds((target_chunks + 1) * EDGE, EDGE)
                elif chunk > target_chunks:
                    continue
            dst[pl.ds(src.shape[0], TILE), at] = placed[x * TILE : (x + 1) * TILE]

    def shifted(g, s, value):
        rows = value.shape[0]
        g[0, s] = pltpu.roll(value, rows - 1, 0).astype(BF16)
        g[1, s] = value.astype(BF16)
        g[2, s] = pltpu.roll(value, 1, 0).astype(BF16)

    r, s_ = iota2(coarse_rows, coarse_rows)
    mean_rows = as_bf16(r // 2 == s_ // 2, 0.25)
    r, s_ = iota2(coarse_rows, t2.shape[0])
    spread_two = as_bf16(coarser(r, coarse) == s_)

    batch = 4

    def top(b, carry):
        x = e4[:, tile_at(2 * batch * b, 2 * batch)]
        means = dot(mean_rows, jnp.maximum(x, jnp.zeros_like(x)))
        wanted = dot(spread_two, t2[:, tile_at(batch * b + SIDE // 2, batch)])
        for u in range(batch):
            one_, two = (means[:, (2 * u + n) * LANES : (2 * u + n + 1) * LANES] for n in (0, 1))
            diff = 0.25 * (one_ + two - wanted[:, u * LANES : (u + 1) * LANES])
            for n in range(2):
                at = 2 * u + n
                mask = x[:, at * LANES : (at + 1) * LANES].astype(F32) > 0
                shifted(ga, 2 * batch * b + at, jnp.where(mask, diff, 0.0))
        return carry

    lax.fori_loop(0, tiles // (2 * batch), top, 0)

    for s in (2, tiles - 4):
        prepare(s, 1, 0, 0, pool_main)
    prepare(2, (tiles - 4) // 2, frames, coarse, pool_tail)

    def conv(g, weights, group, epilogue):
        rows = g.shape[2]
        pairs = (tiles - 4) // 2

        def step(q, carry):
            base = 2 + 2 * group * q
            lhs = jnp.concatenate(
                [
                    jnp.concatenate(
                        [g[i, base + 2 * u - 1 + k] for i in range(3) for k in range(4)], axis=1
                    )
                    for u in range(group)
                ],
                axis=0,
            )
            result = dot_nt(lhs, weights[...])
            for u in range(group):
                epilogue(base + 2 * u, result[u * rows : (u + 1) * rows])
            return carry

        lax.fori_loop(0, pairs // group, step, 0)

    def third(s, value):
        x = e3[:, tile_at(s, 2)].astype(F32)
        masked = jnp.where(x > 0, value, 0.0)
        for n in range(2):
            shifted(gb, s + n, masked[:, n * LANES : (n + 1) * LANES])

    conv(ga, w4, 6, third)

    r, s_ = iota2(fine_rows, coarse_rows)
    spread_rows = as_bf16(coarser(r, frames) == s_)

    def second(s, value):
        x = e2[:, tile_at(s, 2)].astype(F32)
        parts = []
        for n in range(2):
            lanes = slice(n * LANES, (n + 1) * LANES)
            parts.append((0.25 * value[:, lanes] + pre[s + n]).astype(BF16))
        fine = dot(spread_rows, jnp.concatenate(parts, axis=1))
        masked = jnp.where(x > 0, fine, 0.0)
        for n in range(2):
            shifted(gc, s + n, masked[:, n * LANES : (n + 1) * LANES])

    conv(gb, w3, 6, second)

    def first(s, value):
        x = e1[:, tile_at(s, 2)].astype(F32)
        masked = jnp.where(x > 0, value, 0.0).astype(BF16)
        for n in range(2):
            gd[s + n] = masked[:, n * LANES : (n + 1) * LANES]

    conv(gc, w2, 3, first)

    total = jnp.zeros((fine_rows, 4 * mels), F32)
    span = 12
    for s in range(2, tiles - 2, span):
        total += dot_nt(
            jnp.concatenate([gd[s + k] for k in range(span)], axis=1),
            jnp.concatenate([wb[s + k] for k in range(span)], axis=1),
        )
    left, right = total[:, : 2 * mels], total[:, 2 * mels :]
    grad_log = (
        pltpu.roll(left, fine_rows - 1, 0) + pltpu.roll(left, mels, 1) + pltpu.roll(right, 1, 0)
    )[:frames, :mels]
    mel_out[...] = (jnp.concatenate([grad_log, grad_log], axis=1) * gain[...]).astype(BF16)
    mel_copies = exchange(mel_out, mel_in, mel_send, mel_recv)

    for dt, dm, copy in halo:
        pl.when(has(dt, dm))(copy.wait_send)
    finish(spec_copies)
    loads[13].wait()
    finish(mel_copies)

    whole = jnp.concatenate(
        [mel_in[2 * a] + mel_in[2 * a + 1] for a in range(n_mel // 2)], axis=1
    )
    power = dot_nt(whole, filters_b[...])
    grads = []
    for part in range(2):
        for j in range(n_mel):
            spec = spec_in[j, :, pl.ds(part * per, per)].astype(F32)
            grads.append((power[:, j * per : (j + 1) * per] * spec).astype(BF16))
    made = dot(jnp.concatenate(grads, axis=1), table_v[...])
    hop = made.shape[1] // 2
    blocks = made[:, :hop] + pltpu.roll(made[:, hop:], 1, 0)
    for a in range(hop // LANES):
        out[pl.ds(a, share, stride=hop // LANES), :] = blocks[
            :share, a * LANES : (a + 1) * LANES
        ]


def shards(
    act_one,
    act_two,
    act_three,
    act_four,
    target_one,
    target_two,
    kernel_one,
    kernel_two,
    kernel_three,
    kernel_four,
    mel_power,
    loudness,
    filters,
    spec_real,
    spec_imag,
):
    n_tm, n_mel = lax.axis_size("tm"), lax.axis_size("mel")
    frames, mels = mel_power.shape
    bins = filters.shape[0]
    table = jnp.asarray(synthesis_table(bins))
    share = frames // n_mel
    ext = lambda a: pltpu.VMEM((a.shape[0] + TILE, a.shape[1] + 2 * EDGE), BF16)
    length = act_one.shape[1]
    tiles = (length + 2 * EDGE) // LANES
    fine_rows, coarse_rows = frames + TILE, frames // 2 + TILE
    any_spec = pl.BlockSpec(memory_space=pl.ANY)
    vmem = pl.BlockSpec(memory_space=pltpu.VMEM)
    result = pl.pallas_call(
        functools.partial(kernel, n_tm, n_mel),
        out_shape=jax.ShapeDtypeStruct((share * bins // LANES, LANES), F32),
        in_specs=[any_spec] * 8 + [vmem] + [any_spec] * 4 + [vmem] + [any_spec] * 2,
        out_specs=vmem,
        scratch_shapes=[
            ext(act_one),
            ext(act_two),
            ext(act_three),
            ext(act_four),
            ext(target_one),
            ext(target_two),
            pltpu.VMEM(filters.shape, F32),
            pltpu.VMEM(table.shape, BF16),
            pltpu.VMEM((2, TILE, length), BF16),
            pltpu.VMEM((2, TILE, length + 2 * EDGE), BF16),
            pltpu.VMEM((3, tiles, coarse_rows, LANES), BF16),
            pltpu.VMEM((3, tiles, coarse_rows, LANES), BF16),
            pltpu.VMEM((3, tiles, fine_rows, LANES), BF16),
            pltpu.VMEM((tiles, fine_rows, LANES), BF16),
            pltpu.VMEM((tiles, coarse_rows, LANES), F32),
            pltpu.VMEM((frames, 2 * mels), F32),
            pltpu.VMEM(filters.shape, BF16),
            pltpu.VMEM(kernel_two.shape, BF16),
            pltpu.VMEM(kernel_three.shape, BF16),
            pltpu.VMEM(kernel_four.shape, BF16),
            pltpu.VMEM((mels, frames), F32),
            pltpu.VMEM(spec_real.shape, F32),
            pltpu.VMEM(spec_imag.shape, F32),
            pltpu.VMEM((2 * LANES, 12 * LANES), BF16),
            pltpu.VMEM((2 * LANES, 12 * LANES), BF16),
            pltpu.VMEM((2 * LANES, 12 * LANES), BF16),
            pltpu.VMEM((tiles, 4 * mels, LANES), BF16),
            pltpu.VMEM((frames, 2 * spec_real.shape[1]), BF16),
            pltpu.VMEM((n_mel, share + TILE, 2 * spec_real.shape[1]), BF16),
            pltpu.VMEM((frames, 2 * mels), BF16),
            pltpu.VMEM((n_mel, share + TILE, 2 * mels), BF16),
            pltpu.SemaphoreType.DMA((14,)),
            pltpu.SemaphoreType.DMA((18,)),
            pltpu.SemaphoreType.DMA((18,)),
            pltpu.SemaphoreType.DMA((2 * n_mel,)),
            pltpu.SemaphoreType.DMA((2 * n_mel,)),
            pltpu.SemaphoreType.DMA((2 * n_mel,)),
            pltpu.SemaphoreType.DMA((2 * n_mel,)),
        ],
        compiler_params=pltpu.CompilerParams(
            collective_id=0, has_side_effects=True, vmem_limit_bytes=56 * 2**20
        ),
        name="wave_gradient",
    )(
        act_one,
        act_two,
        act_three,
        act_four,
        target_one,
        target_two,
        filters,
        table,
        jnp.transpose(kernel_one, (0, 2, 1, 3)).reshape(3, 3, kernel_one.shape[3]),
        kernel_two,
        kernel_three,
        kernel_four,
        mel_power.T,
        loudness.reshape(1, mels),
        spec_real,
        spec_imag,
    )
    return result.reshape(-1)


def solution(mesh):
    return jax.shard_map(
        shards,
        mesh=mesh,
        in_specs=(
            P("tm", "mel"),
            P("tm", "mel"),
            P("tm", "mel"),
            P("tm", "mel"),
            P("tm", "mel"),
            P("tm", "mel"),
            P(),
            P(),
            P(),
            P(),
            P("tm", "mel"),
            P("mel"),
            P(),
            P("tm", "mel"),
            P("tm", "mel"),
        ),
        out_specs=P(("tm", "mel")),
        check_vma=False,
    )
```

```python
import functools

import jax
import jax.numpy as jnp
import ml_dtypes
import numpy as np
from jax import lax
from jax.experimental import pallas as pl
from jax.experimental.pallas import tpu as pltpu
from jax.sharding import PartitionSpec as P

LANES = 128
TILE = 16
SIDE = 4
EDGE = SIDE * LANES
MESH = pl.DeviceIdType.MESH
BF16 = jnp.bfloat16
F32 = jnp.float32

DEPTH = (1, 2, 2, 4, 1, 2)
PLACE = (0, 1, 3, 5, 9, 10)
WIDTH = (128, 128, 256, 512, 128, 256)
GROUPS = ((3, 5), (2, 1, 0, 4))


def synthesis_table(bins):
    points = 2 * bins
    sample = np.arange(points)
    angle = (np.arange(bins)[:, None] * sample[None, :] % points) * (2.0 * np.pi / points)
    window = 0.5 - 0.5 * np.cos(sample * (2.0 * np.pi / points))
    scale = 2.0 * window * points**-0.5
    table = np.concatenate([np.cos(angle) * scale, -np.sin(angle) * scale], axis=0)
    return table.astype(np.float32).astype(ml_dtypes.bfloat16)


def iota2(rows, cols):
    return (
        lax.broadcasted_iota(jnp.int32, (rows, cols), 0),
        lax.broadcasted_iota(jnp.int32, (rows, cols), 1),
    )


def as_bf16(mask, value=1.0):
    return jnp.where(mask, value, 0.0).astype(F32).astype(BF16)


def coarser(row, main):
    return row // 2 + jnp.where(row >= main + TILE // 2, TILE // 2, 0)


def dot(a, b):
    return jnp.dot(a, b, preferred_element_type=F32)


def dot_nt(a, b):
    return lax.dot_general(a, b, (((1,), (1,)), ((), ())), preferred_element_type=F32)


def kernel(
    n_tm,
    n_mel,
    act_one,
    act_two,
    act_three,
    act_four,
    target_one,
    target_two,
    filters,
    table,
    kernel_one,
    kernel_two,
    kernel_three,
    kernel_four,
    mel_power,
    loudness,
    spec_real,
    spec_imag,
    out,
    e1,
    e2,
    e3,
    e4,
    t1,
    t2,
    filters_v,
    table_v,
    pack_out,
    pack_in,
    corner_out,
    corner_in,
    ga,
    gb,
    gc,
    gd,
    pre,
    gain,
    filters_b,
    k2_v,
    k3_v,
    k4_v,
    power_v,
    real_v,
    imag_v,
    w4,
    w3,
    w2,
    wb,
    spec_out,
    spec_in,
    mel_out,
    mel_in,
    load_sem,
    halo_send,
    halo_recv,
    spec_send,
    spec_recv,
    mel_send,
    mel_recv,
):
    tm, mel = lax.axis_index("tm"), lax.axis_index("mel")
    length = act_one.shape[1]
    inputs = (act_one, act_two, act_three, act_four, target_one, target_two)
    wide = (e1, e2, e3, e4, t1, t2)
    frames, coarse = act_one.shape[0], act_three.shape[0]
    fine_rows, coarse_rows = e1.shape[0], e3.shape[0]
    tiles = e1.shape[1] // LANES
    share = frames // n_mel

    loads = []
    for at, (src, dst) in enumerate(zip(inputs, wide)):
        rows, cols = src.shape
        loads.append(
            pltpu.make_async_copy(
                src, dst.at[pl.ds(0, rows), pl.ds(EDGE, cols)], load_sem.at[at]
            )
        )
    for src, dst in (
        (kernel_two, k2_v),
        (kernel_three, k3_v),
        (kernel_four, k4_v),
        (mel_power, power_v),
        (spec_real, real_v),
        (spec_imag, imag_v),
        (filters, filters_v),
        (table, table_v),
    ):
        loads.append(pltpu.make_async_copy(src, dst, load_sem.at[len(loads)]))
    for load in loads:
        load.start()

    for src, dst in zip(inputs, wide):
        rows, cols = src.shape
        dst[pl.ds(0, rows), pl.ds(0, EDGE)] = jnp.zeros((rows, EDGE), BF16)
        dst[pl.ds(0, rows), pl.ds(EDGE + cols, EDGE)] = jnp.zeros((rows, EDGE), BF16)
    pack_in[...] = jnp.zeros(pack_in.shape, BF16)
    corner_in[...] = jnp.zeros(corner_in.shape, BF16)
    spec_in[...] = jnp.zeros(spec_in.shape, BF16)
    mel_in[...] = jnp.zeros(mel_in.shape, BF16)

    barrier = pltpu.get_barrier_semaphore()

    def has(dt, dm):
        cond = jnp.bool_(True)
        if dt:
            cond = (tm > 0) if dt < 0 else (tm < n_tm - 1)
        if dm:
            side = (mel > 0) if dm < 0 else (mel < n_mel - 1)
            cond = side if not dt else jnp.logical_and(cond, side)
        return cond

    for dt in (-1, 0, 1):
        for k in range(n_mel):
            if dt == 0 and k == 0:
                continue

            def greet(dt=dt, k=k):
                pl.semaphore_signal(
                    barrier,
                    inc=1,
                    device_id={"tm": tm + dt, "mel": lax.rem(mel + k, n_mel)},
                    device_id_type=MESH,
                )

            if dt:
                pl.when(has(dt, 0))(greet)
            else:
                greet()

    halo = []

    def add_halo(dt, dm, src, dst):
        at = len(halo)
        copy = pltpu.make_async_remote_copy(
            src_ref=src,
            dst_ref=dst,
            send_sem=halo_send.at[at],
            recv_sem=halo_recv.at[at],
            device_id={"tm": tm + dt, "mel": mel + dm},
            device_id_type=MESH,
        )
        halo.append((dt, dm, copy))
        pl.when(has(dt, dm))(copy.start)

    def exchange(src, dst, send, recv):
        copies = []
        for k in range(n_mel):
            j = lax.rem(mel + k, n_mel)
            main = pl.ds(pl.multiple_of(j * share, TILE), share)
            before = pl.ds(
                pl.multiple_of(lax.rem(j * share + frames - TILE, frames), TILE), TILE
            )
            if k:
                copy = pltpu.make_async_remote_copy(
                    src_ref=src.at[main],
                    dst_ref=dst.at[mel, pl.ds(0, share)],
                    send_sem=send.at[k],
                    recv_sem=recv.at[k],
                    device_id={"tm": tm, "mel": j},
                    device_id_type=MESH,
                )
                copy.start()
                copies.append((copy, None, None))
            copy = pltpu.make_async_remote_copy(
                src_ref=src.at[before],
                dst_ref=dst.at[mel, pl.ds(share, TILE)],
                send_sem=send.at[n_mel + k],
                recv_sem=recv.at[n_mel + k],
                device_id={"tm": tm + jnp.where(j == 0, 1, 0), "mel": j},
                device_id_type=MESH,
            )
            if k:
                sends = jnp.logical_or(j > 0, tm < n_tm - 1)
                receives = jnp.logical_or(mel > 0, tm > 0)
            else:
                sends = jnp.logical_and(mel == 0, tm < n_tm - 1)
                receives = jnp.logical_and(mel == 0, tm > 0)
            pl.when(sends)(copy.start)
            copies.append((copy, sends, receives))
        dst[mel, pl.ds(0, share)] = src[pl.ds(pl.multiple_of(mel * share, TILE), share)]

        @pl.when(mel > 0)
        def _():
            dst[mel, pl.ds(share, TILE)] = src[
                pl.ds(pl.multiple_of(mel * share - TILE, TILE), TILE)
            ]

        return copies

    def finish(copies):
        for copy, sends, receives in copies:
            if sends is None:
                copy.wait_recv()
            else:
                pl.when(receives)(copy.wait_recv)
        for copy, sends, receives in copies:
            if sends is None:
                copy.wait_send()
            else:
                pl.when(sends)(copy.wait_send)

    for load in loads[:6]:
        load.wait()
    o, c = iota2(TILE, 6 * TILE)
    first_rows = jnp.zeros((TILE, 6 * TILE), jnp.bool_)
    last_rows = jnp.zeros((TILE, 6 * TILE), jnp.bool_)
    for x in range(6):
        inside = (o >= PLACE[x]) & (o < PLACE[x] + DEPTH[x])
        first_rows |= inside & (c - x * TILE == o - PLACE[x])
        last_rows |= inside & (c - x * TILE - (TILE - DEPTH[x]) == o - PLACE[x])
    picks = (as_bf16(first_rows), as_bf16(last_rows))
    counts = [src.shape[1] // EDGE for src in inputs]

    def tail_parts(x, end, chunks):
        src, dst = inputs[x], wide[x]
        row = src.shape[0] - TILE if end else 0
        return [dst[pl.ds(row, TILE), pl.ds(EDGE + at * EDGE, EDGE)] for at in chunks]

    def travels(group, end, o, k):
        found = jnp.zeros(o.shape, jnp.bool_)
        first = base = 0
        for x in group:
            inner = k - first
            row = inner % TILE - (TILE - DEPTH[x] if end else 0)
            found |= (
                (inner >= 0)
                & (inner < counts[x] * TILE)
                & (row >= 0)
                & (row < DEPTH[x])
                & (o == base + DEPTH[x] * (inner // TILE) + row)
            )
            first += counts[x] * TILE
            base += counts[x] * DEPTH[x]
        return found

    pack_rows = pack_out.shape[2]
    for g, group in enumerate(GROUPS):
        o, k = iota2(pack_rows, sum(counts[x] for x in group) * TILE)
        for end in (0, 1):
            parts = [p for x in group for p in tail_parts(x, end, range(counts[x]))]
            pack_out[g, end] = dot(
                as_bf16(travels(group, end, o, k)), jnp.concatenate(parts, axis=0)
            ).astype(BF16)
    for end in (0, 1):
        for side in (0, 1):
            parts = [
                p for x in range(6) for p in tail_parts(x, end, [counts[x] - 1 if side else 0])
            ]
            corner_out[end, side] = dot(picks[end], jnp.concatenate(parts, axis=0)).astype(BF16)
    for load in loads[10:12]:
        load.wait()
    per = spec_real.shape[1]
    spec_out[:, pl.ds(0, per)] = real_v[...].astype(BF16)
    spec_out[:, pl.ds(per, per)] = imag_v[...].astype(BF16)

    rows_of_peers = 1 + jnp.where(tm > 0, 1, 0) + jnp.where(tm < n_tm - 1, 1, 0)
    pl.semaphore_wait(barrier, n_mel * rows_of_peers - 1)
    ends = ((1, 1), (0, -1))

    def lateral(x):
        src, dst, width = inputs[x], wide[x], WIDTH[x]
        rows, cols = src.shape
        add_halo(
            0,
            1,
            src.at[:, pl.ds(cols - width, width)],
            dst.at[pl.ds(0, rows), pl.ds(EDGE - width, width)],
        )
        add_halo(
            0,
            -1,
            src.at[:, pl.ds(0, width)],
            dst.at[pl.ds(0, rows), pl.ds(EDGE + cols, width)],
        )

    for end, dt in ends:
        add_halo(dt, 0, pack_out.at[0, end], pack_in.at[0, 1 - end])
    for x in GROUPS[0]:
        lateral(x)
    for end, dt in ends:
        add_halo(dt, 1, corner_out.at[end, 1], corner_in.at[1 - end, 0])
        add_halo(dt, -1, corner_out.at[end, 0], corner_in.at[1 - end, 1])
    needed_first = len(halo)
    for end, dt in ends:
        add_halo(dt, 0, pack_out.at[1, end], pack_in.at[1, 1 - end])
    for x in GROUPS[1]:
        lateral(x)
    spec_copies = exchange(spec_out, spec_in, spec_send, spec_recv)

    for load in loads[6:10]:
        load.wait()
    w4[...] = jnp.zeros(w4.shape, BF16)
    w3[...] = jnp.zeros(w3.shape, BF16)
    half = LANES // 2
    blank = jnp.zeros((half, half), F32)
    for i in range(3):
        for k in range(4):
            lanes = pl.ds((i * 4 + k) * LANES, LANES)
            for n in range(2):
                j = n - (k - 1)
                if abs(j) <= 1:
                    w4[pl.ds(n * LANES, LANES), lanes] = k4_v[i, j + 1]
                    w3[pl.ds(n * LANES, half), lanes] = k3_v[i, j + 1]
                    w3[pl.ds(n * LANES + half, half), lanes] = k3_v[i, j + 1]
                for a in range(2):
                    pair = []
                    for b in range(2):
                        j = (2 * n + a) - (2 * (k - 1) + b)
                        pair.append(
                            k2_v[i, j + 1].astype(F32) if abs(j) <= 1 else blank
                        )
                    w2[pl.ds(n * LANES + a * half, half), lanes] = jnp.concatenate(
                        pair, axis=1
                    ).astype(BF16)
    mels = mel_power.shape[0]
    one = kernel_one[...].astype(F32)
    one = jnp.concatenate([one, one], axis=2)
    m, lane = iota2(mels, LANES)

    def band(s, carry):
        d = m - (2 * (s - SIDE) + lane // half)
        for i in range(3):
            value = jnp.zeros((mels, LANES), F32)
            for j in range(3):
                value = jnp.where(d == j - 1, one[i, j][None, :], value)
            wb[s, pl.ds(i * mels, mels)] = value.astype(BF16)
        wb[s, pl.ds(3 * mels, mels)] = jnp.zeros((mels, LANES), BF16)
        return carry

    lax.fori_loop(2, tiles - 2, band, 0)
    for g in (gb, gc):
        for s in (1, tiles - 2):
            for i in range(3):
                g[i, s] = jnp.zeros(g.shape[2:], BF16)

    loud = loudness[...]
    level = loud / (1.0 + loud * jnp.transpose(power_v[...]))
    level = jnp.concatenate([level, level], axis=1)
    lane = lax.broadcasted_iota(jnp.int32, level.shape, 1)
    gain[...] = jnp.where(lane // mels == lax.rem(mel, 2), level, 0.0)
    loads[12].wait()
    filters_b[...] = filters_v[...].astype(BF16)

    def tile_at(s, count=1):
        return pl.ds(pl.multiple_of(s * LANES, LANES), count * LANES)

    def prepare(s, pairs, fine_at, coarse_at, matrix):
        rows_at = pl.ds(coarse_at, matrix.shape[0])
        x = e2[pl.ds(fine_at, matrix.shape[1]), tile_at(s, 2 * pairs)]
        sums = dot(matrix, jnp.maximum(x, jnp.zeros_like(x)))
        low = lax.broadcasted_iota(jnp.int32, (matrix.shape[0], LANES), 1) < half
        for u in range(pairs):
            want = t1[rows_at, tile_at((s - SIDE) // 2 + SIDE + u)].astype(F32)
            turned = pltpu.roll(want, half, 1)
            wants = (jnp.where(low, want, turned), jnp.where(low, turned, want))
            for n in range(2):
                at = 2 * u + n
                block = sums[:, at * LANES : (at + 1) * LANES]
                pre[s + at, rows_at] = 0.25 * (block + pltpu.roll(block, half, 1) - wants[n])

    r, s_ = iota2(coarse, frames)
    pool_main = as_bf16(s_ // 2 == r, 0.25)
    r, s_ = iota2(TILE, TILE)
    pool_tail = as_bf16(coarser(s_, 0) == r, 0.25)

    def early(q, carry):
        prepare(SIDE + 8 * q, 4, 0, 0, pool_main)
        return carry

    lax.fori_loop(0, (tiles - 2 * SIDE) // 8, early, 0)

    def arrive(g):
        for dt, dm, copy in halo[needed_first:] if g else halo[:needed_first]:
            pl.when(has(-dt, -dm))(copy.wait_recv)
        group = GROUPS[g]
        k, o = iota2(sum(counts[x] for x in group) * TILE, pack_rows)
        spots = jnp.concatenate(
            [as_bf16(travels(group, 1, o, k)), as_bf16(travels(group, 0, o, k))], axis=1
        )
        both = jnp.concatenate([pack_in[g, 0], pack_in[g, 1]], axis=0)
        placed = dot(spots, both).astype(BF16)
        first = 0
        for x in group:
            for at in range(counts[x]):
                wide[x][pl.ds(inputs[x].shape[0], TILE), pl.ds(EDGE + at * EDGE, EDGE)] = placed[
                    first : first + TILE
                ]
                first += TILE

    arrive(0)
    o, c = iota2(6 * TILE, 2 * TILE)
    spots = jnp.zeros((6 * TILE, 2 * TILE), jnp.bool_)
    for x in range(6):
        for at, base in ((0, TILE - DEPTH[x]), (1, 0)):
            r, p = o - x * TILE - base, c - at * TILE - PLACE[x]
            spots |= (r == p) & (r >= 0) & (r < DEPTH[x])
    spots = as_bf16(spots)
    for side in (0, 1):
        both = jnp.concatenate([corner_in[0, side], corner_in[1, side]], axis=0)
        placed = dot(spots, both).astype(BF16)
        for x, (src, dst) in enumerate(zip(inputs, wide)):
            at = pl.ds((counts[x] + 1) * EDGE if side else 0, EDGE)
            dst[pl.ds(src.shape[0], TILE), at] = placed[x * TILE : (x + 1) * TILE]

    def shifted(g, s, value):
        rows = value.shape[0]
        g[0, s] = pltpu.roll(value, rows - 1, 0).astype(BF16)
        g[1, s] = value.astype(BF16)
        g[2, s] = pltpu.roll(value, 1, 0).astype(BF16)

    r, s_ = iota2(coarse_rows, coarse_rows)
    mean_rows = as_bf16(r // 2 == s_ // 2, 0.25)
    r, s_ = iota2(coarse_rows, t2.shape[0])
    spread_two = as_bf16(coarser(r, coarse) == s_)

    batch = 4

    def top(b, carry):
        x = e4[:, tile_at(2 * batch * b, 2 * batch)]
        means = dot(mean_rows, jnp.maximum(x, jnp.zeros_like(x)))
        wanted = dot(spread_two, t2[:, tile_at(batch * b + SIDE // 2, batch)])
        for u in range(batch):
            one_, two = (means[:, (2 * u + n) * LANES : (2 * u + n + 1) * LANES] for n in (0, 1))
            diff = 0.25 * (one_ + two - wanted[:, u * LANES : (u + 1) * LANES])
            for n in range(2):
                at = 2 * u + n
                mask = x[:, at * LANES : (at + 1) * LANES].astype(F32) > 0
                shifted(ga, 2 * batch * b + at, jnp.where(mask, diff, 0.0))
        return carry

    lax.fori_loop(0, tiles // (2 * batch), top, 0)

    arrive(1)
    for s in (2, tiles - 4):
        prepare(s, 1, 0, 0, pool_main)
    prepare(2, (tiles - 4) // 2, frames, coarse, pool_tail)

    def conv(g, weights, group, epilogue):
        rows = g.shape[2]
        pairs = (tiles - 4) // 2

        def step(q, carry):
            base = 2 + 2 * group * q
            lhs = jnp.concatenate(
                [
                    jnp.concatenate(
                        [g[i, base + 2 * u - 1 + k] for i in range(3) for k in range(4)], axis=1
                    )
                    for u in range(group)
                ],
                axis=0,
            )
            result = dot_nt(lhs, weights[...])
            for u in range(group):
                epilogue(base + 2 * u, result[u * rows : (u + 1) * rows])
            return carry

        lax.fori_loop(0, pairs // group, step, 0)

    def third(s, value):
        x = e3[:, tile_at(s, 2)].astype(F32)
        masked = jnp.where(x > 0, value, 0.0)
        for n in range(2):
            shifted(gb, s + n, masked[:, n * LANES : (n + 1) * LANES])

    conv(ga, w4, 6, third)

    r, s_ = iota2(fine_rows, coarse_rows)
    spread_rows = as_bf16(coarser(r, frames) == s_)

    def second(s, value):
        x = e2[:, tile_at(s, 2)].astype(F32)
        parts = []
        for n in range(2):
            lanes = slice(n * LANES, (n + 1) * LANES)
            parts.append((0.25 * value[:, lanes] + pre[s + n]).astype(BF16))
        fine = dot(spread_rows, jnp.concatenate(parts, axis=1))
        masked = jnp.where(x > 0, fine, 0.0)
        for n in range(2):
            shifted(gc, s + n, masked[:, n * LANES : (n + 1) * LANES])

    conv(gb, w3, 6, second)

    def first(s, value):
        x = e1[:, tile_at(s, 2)].astype(F32)
        masked = jnp.where(x > 0, value, 0.0).astype(BF16)
        for n in range(2):
            gd[s + n] = masked[:, n * LANES : (n + 1) * LANES]

    conv(gc, w2, 3, first)

    total = jnp.zeros((fine_rows, 4 * mels), F32)
    span = 12
    for s in range(2, tiles - 2, span):
        total += dot_nt(
            jnp.concatenate([gd[s + k] for k in range(span)], axis=1),
            jnp.concatenate([wb[s + k] for k in range(span)], axis=1),
        )
    left, right = total[:, : 2 * mels], total[:, 2 * mels :]
    grad_log = (
        pltpu.roll(left, fine_rows - 1, 0) + pltpu.roll(left, mels, 1) + pltpu.roll(right, 1, 0)
    )[:frames, :mels]
    mel_out[...] = (jnp.concatenate([grad_log, grad_log], axis=1) * gain[...]).astype(BF16)
    mel_copies = exchange(mel_out, mel_in, mel_send, mel_recv)

    for dt, dm, copy in halo:
        pl.when(has(dt, dm))(copy.wait_send)
    finish(spec_copies)
    loads[13].wait()
    finish(mel_copies)

    whole = jnp.concatenate(
        [mel_in[2 * a] + mel_in[2 * a + 1] for a in range(n_mel // 2)], axis=1
    )
    power = dot_nt(whole, filters_b[...])
    grads = []
    for part in range(2):
        for j in range(n_mel):
            spec = spec_in[j, :, pl.ds(part * per, per)].astype(F32)
            grads.append((power[:, j * per : (j + 1) * per] * spec).astype(BF16))
    made = dot(jnp.concatenate(grads, axis=1), table_v[...])
    hop = made.shape[1] // 2
    blocks = made[:, :hop] + pltpu.roll(made[:, hop:], 1, 0)
    for a in range(hop // LANES):
        out[pl.ds(a, share, stride=hop // LANES), :] = blocks[
            :share, a * LANES : (a + 1) * LANES
        ]


def shards(
    act_one,
    act_two,
    act_three,
    act_four,
    target_one,
    target_two,
    kernel_one,
    kernel_two,
    kernel_three,
    kernel_four,
    mel_power,
    loudness,
    filters,
    spec_real,
    spec_imag,
):
    n_tm, n_mel = lax.axis_size("tm"), lax.axis_size("mel")
    frames, mels = mel_power.shape
    bins = filters.shape[0]
    table = jnp.asarray(synthesis_table(bins))
    share = frames // n_mel
    ext = lambda a: pltpu.VMEM((a.shape[0] + TILE, a.shape[1] + 2 * EDGE), BF16)
    length = act_one.shape[1]
    tiles = (length + 2 * EDGE) // LANES
    fine_rows, coarse_rows = frames + TILE, frames // 2 + TILE
    arrays = (act_one, act_two, act_three, act_four, target_one, target_two)
    pack_rows = max(
        sum(DEPTH[x] * (arrays[x].shape[1] // EDGE) for x in group) for group in GROUPS
    )
    pack_rows = -(-pack_rows // TILE) * TILE
    any_spec = pl.BlockSpec(memory_space=pl.ANY)
    vmem = pl.BlockSpec(memory_space=pltpu.VMEM)
    result = pl.pallas_call(
        functools.partial(kernel, n_tm, n_mel),
        out_shape=jax.ShapeDtypeStruct((share * bins // LANES, LANES), F32),
        in_specs=[any_spec] * 8 + [vmem] + [any_spec] * 4 + [vmem] + [any_spec] * 2,
        out_specs=vmem,
        scratch_shapes=[
            ext(act_one),
            ext(act_two),
            ext(act_three),
            ext(act_four),
            ext(target_one),
            ext(target_two),
            pltpu.VMEM(filters.shape, F32),
            pltpu.VMEM(table.shape, BF16),
            pltpu.VMEM((2, 2, pack_rows, EDGE), BF16),
            pltpu.VMEM((2, 2, pack_rows, EDGE), BF16),
            pltpu.VMEM((2, 2, TILE, EDGE), BF16),
            pltpu.VMEM((2, 2, TILE, EDGE), BF16),
            pltpu.VMEM((3, tiles, coarse_rows, LANES), BF16),
            pltpu.VMEM((3, tiles, coarse_rows, LANES), BF16),
            pltpu.VMEM((3, tiles, fine_rows, LANES), BF16),
            pltpu.VMEM((tiles, fine_rows, LANES), BF16),
            pltpu.VMEM((tiles, coarse_rows, LANES), F32),
            pltpu.VMEM((frames, 2 * mels), F32),
            pltpu.VMEM(filters.shape, BF16),
            pltpu.VMEM(kernel_two.shape, BF16),
            pltpu.VMEM(kernel_three.shape, BF16),
            pltpu.VMEM(kernel_four.shape, BF16),
            pltpu.VMEM((mels, frames), F32),
            pltpu.VMEM(spec_real.shape, F32),
            pltpu.VMEM(spec_imag.shape, F32),
            pltpu.VMEM((2 * LANES, 12 * LANES), BF16),
            pltpu.VMEM((2 * LANES, 12 * LANES), BF16),
            pltpu.VMEM((2 * LANES, 12 * LANES), BF16),
            pltpu.VMEM((tiles, 4 * mels, LANES), BF16),
            pltpu.VMEM((frames, 2 * spec_real.shape[1]), BF16),
            pltpu.VMEM((n_mel, share + TILE, 2 * spec_real.shape[1]), BF16),
            pltpu.VMEM((frames, 2 * mels), BF16),
            pltpu.VMEM((n_mel, share + TILE, 2 * mels), BF16),
            pltpu.SemaphoreType.DMA((14,)),
            pltpu.SemaphoreType.DMA((20,)),
            pltpu.SemaphoreType.DMA((20,)),
            pltpu.SemaphoreType.DMA((2 * n_mel,)),
            pltpu.SemaphoreType.DMA((2 * n_mel,)),
            pltpu.SemaphoreType.DMA((2 * n_mel,)),
            pltpu.SemaphoreType.DMA((2 * n_mel,)),
        ],
        compiler_params=pltpu.CompilerParams(
            collective_id=0, has_side_effects=True, vmem_limit_bytes=56 * 2**20
        ),
        name="wave_gradient",
    )(
        act_one,
        act_two,
        act_three,
        act_four,
        target_one,
        target_two,
        filters,
        table,
        jnp.transpose(kernel_one, (0, 2, 1, 3)).reshape(3, 3, kernel_one.shape[3]),
        kernel_two,
        kernel_three,
        kernel_four,
        mel_power.T,
        loudness.reshape(1, mels),
        spec_real,
        spec_imag,
    )
    return result.reshape(-1)


def solution(mesh):
    return jax.shard_map(
        shards,
        mesh=mesh,
        in_specs=(
            P("tm", "mel"),
            P("tm", "mel"),
            P("tm", "mel"),
            P("tm", "mel"),
            P("tm", "mel"),
            P("tm", "mel"),
            P(),
            P(),
            P(),
            P(),
            P("tm", "mel"),
            P("mel"),
            P(),
            P("tm", "mel"),
            P("tm", "mel"),
        ),
        out_specs=P(("tm", "mel")),
        check_vma=False,
    )
```

```python
import functools

import jax
import jax.numpy as jnp
import ml_dtypes
import numpy as np
from jax import lax
from jax.experimental import pallas as pl
from jax.experimental.pallas import tpu as pltpu
from jax.sharding import PartitionSpec as P

LANES = 128
TILE = 16
SIDE = 4
EDGE = SIDE * LANES
MESH = pl.DeviceIdType.MESH
BF16 = jnp.bfloat16
F32 = jnp.float32

DEPTH = (1, 2, 2, 4, 1, 2)
PLACE = (0, 1, 3, 5, 9, 10)
WIDTH = (128, 128, 256, 512, 128, 256)
GROUPS = ((3, 5), (2, 1, 0, 4))


def synthesis_table(bins):
    points = 2 * bins
    sample = np.arange(points)
    angle = (np.arange(bins)[:, None] * sample[None, :] % points) * (2.0 * np.pi / points)
    window = 0.5 - 0.5 * np.cos(sample * (2.0 * np.pi / points))
    scale = 2.0 * window * points**-0.5
    table = np.concatenate([np.cos(angle) * scale, -np.sin(angle) * scale], axis=0)
    return table.astype(np.float32).astype(ml_dtypes.bfloat16)


def iota2(rows, cols):
    return (
        lax.broadcasted_iota(jnp.int32, (rows, cols), 0),
        lax.broadcasted_iota(jnp.int32, (rows, cols), 1),
    )


def as_bf16(mask, value=1.0):
    return jnp.where(mask, value, 0.0).astype(F32).astype(BF16)


def coarser(row, main):
    return row // 2 + jnp.where(row >= main + TILE // 2, TILE // 2, 0)


def dot(a, b):
    return jnp.dot(a, b, preferred_element_type=F32)


def dot_nt(a, b):
    return lax.dot_general(a, b, (((1,), (1,)), ((), ())), preferred_element_type=F32)


def kernel(
    n_tm,
    n_mel,
    act_one,
    act_two,
    act_three,
    act_four,
    target_one,
    target_two,
    filters,
    table,
    kernel_one,
    kernel_two,
    kernel_three,
    kernel_four,
    mel_power,
    loudness,
    spec_real,
    spec_imag,
    out,
    e1,
    e2,
    e3,
    e4,
    t1,
    t2,
    filters_v,
    table_v,
    pack_out,
    pack_in,
    corner_out,
    corner_in,
    ga,
    gb,
    gc,
    gd,
    pre,
    gain,
    filters_b,
    k2_v,
    k3_v,
    k4_v,
    power_v,
    real_v,
    imag_v,
    w4,
    w3,
    w2,
    band,
    wb,
    spec_out,
    spec_in,
    mel_out,
    mel_in,
    load_sem,
    halo_send,
    halo_recv,
    spec_send,
    spec_recv,
    mel_send,
    mel_recv,
):
    tm, mel = lax.axis_index("tm"), lax.axis_index("mel")
    length = act_one.shape[1]
    inputs = (act_one, act_two, act_three, act_four, target_one, target_two)
    wide = (e1, e2, e3, e4, t1, t2)
    frames, coarse = act_one.shape[0], act_three.shape[0]
    fine_rows, coarse_rows = e1.shape[0], e3.shape[0]
    tiles = e1.shape[1] // LANES
    share = frames // n_mel

    loads = []
    for at, (src, dst) in enumerate(zip(inputs, wide)):
        rows, cols = src.shape
        loads.append(
            pltpu.make_async_copy(
                src, dst.at[pl.ds(0, rows), pl.ds(EDGE, cols)], load_sem.at[at]
            )
        )
    for src, dst in (
        (kernel_two, k2_v),
        (kernel_three, k3_v),
        (kernel_four, k4_v),
        (mel_power, power_v),
        (spec_real, real_v),
        (spec_imag, imag_v),
        (filters, filters_v),
        (table, table_v),
    ):
        loads.append(pltpu.make_async_copy(src, dst, load_sem.at[len(loads)]))
    for load in loads:
        load.start()

    for src, dst in zip(inputs, wide):
        rows, cols = src.shape
        dst[pl.ds(0, rows), pl.ds(0, EDGE)] = jnp.zeros((rows, EDGE), BF16)
        dst[pl.ds(0, rows), pl.ds(EDGE + cols, EDGE)] = jnp.zeros((rows, EDGE), BF16)
    pack_in[...] = jnp.zeros(pack_in.shape, BF16)
    corner_in[...] = jnp.zeros(corner_in.shape, BF16)
    spec_in[...] = jnp.zeros(spec_in.shape, BF16)
    mel_in[...] = jnp.zeros(mel_in.shape, BF16)

    barrier = pltpu.get_barrier_semaphore()

    def has(dt, dm):
        cond = jnp.bool_(True)
        if dt:
            cond = (tm > 0) if dt < 0 else (tm < n_tm - 1)
        if dm:
            side = (mel > 0) if dm < 0 else (mel < n_mel - 1)
            cond = side if not dt else jnp.logical_and(cond, side)
        return cond

    for dt in (-1, 0, 1):
        for k in range(n_mel):
            if dt == 0 and k == 0:
                continue

            def greet(dt=dt, k=k):
                pl.semaphore_signal(
                    barrier,
                    inc=1,
                    device_id={"tm": tm + dt, "mel": lax.rem(mel + k, n_mel)},
                    device_id_type=MESH,
                )

            if dt:
                pl.when(has(dt, 0))(greet)
            else:
                greet()

    halo = []

    def add_halo(dt, dm, src, dst):
        at = len(halo)
        copy = pltpu.make_async_remote_copy(
            src_ref=src,
            dst_ref=dst,
            send_sem=halo_send.at[at],
            recv_sem=halo_recv.at[at],
            device_id={"tm": tm + dt, "mel": mel + dm},
            device_id_type=MESH,
        )
        halo.append((dt, dm, copy))
        pl.when(has(dt, dm))(copy.start)

    def exchange(src, dst, send, recv):
        copies = []
        for k in range(n_mel):
            j = lax.rem(mel + k, n_mel)
            main = pl.ds(pl.multiple_of(j * share, TILE), share)
            before = pl.ds(
                pl.multiple_of(lax.rem(j * share + frames - TILE, frames), TILE), TILE
            )
            if k:
                copy = pltpu.make_async_remote_copy(
                    src_ref=src.at[main],
                    dst_ref=dst.at[mel, pl.ds(0, share)],
                    send_sem=send.at[k],
                    recv_sem=recv.at[k],
                    device_id={"tm": tm, "mel": j},
                    device_id_type=MESH,
                )
                copy.start()
                copies.append((copy, None, None))
            copy = pltpu.make_async_remote_copy(
                src_ref=src.at[before],
                dst_ref=dst.at[mel, pl.ds(share, TILE)],
                send_sem=send.at[n_mel + k],
                recv_sem=recv.at[n_mel + k],
                device_id={"tm": tm + jnp.where(j == 0, 1, 0), "mel": j},
                device_id_type=MESH,
            )
            if k:
                sends = jnp.logical_or(j > 0, tm < n_tm - 1)
                receives = jnp.logical_or(mel > 0, tm > 0)
            else:
                sends = jnp.logical_and(mel == 0, tm < n_tm - 1)
                receives = jnp.logical_and(mel == 0, tm > 0)
            pl.when(sends)(copy.start)
            copies.append((copy, sends, receives))
        dst[mel, pl.ds(0, share)] = src[pl.ds(pl.multiple_of(mel * share, TILE), share)]

        @pl.when(mel > 0)
        def _():
            dst[mel, pl.ds(share, TILE)] = src[
                pl.ds(pl.multiple_of(mel * share - TILE, TILE), TILE)
            ]

        return copies

    def finish(copies):
        for copy, sends, receives in copies:
            if sends is None:
                copy.wait_recv()
            else:
                pl.when(receives)(copy.wait_recv)
        for copy, sends, receives in copies:
            if sends is None:
                copy.wait_send()
            else:
                pl.when(sends)(copy.wait_send)

    for load in loads[:6]:
        load.wait()
    o, c = iota2(TILE, 6 * TILE)
    first_rows = jnp.zeros((TILE, 6 * TILE), jnp.bool_)
    last_rows = jnp.zeros((TILE, 6 * TILE), jnp.bool_)
    for x in range(6):
        inside = (o >= PLACE[x]) & (o < PLACE[x] + DEPTH[x])
        first_rows |= inside & (c - x * TILE == o - PLACE[x])
        last_rows |= inside & (c - x * TILE - (TILE - DEPTH[x]) == o - PLACE[x])
    picks = (as_bf16(first_rows), as_bf16(last_rows))
    counts = [src.shape[1] // EDGE for src in inputs]

    def tail_parts(x, end, chunks):
        src, dst = inputs[x], wide[x]
        row = src.shape[0] - TILE if end else 0
        return [dst[pl.ds(row, TILE), pl.ds(EDGE + at * EDGE, EDGE)] for at in chunks]

    def travels(group, end, o, k):
        found = jnp.zeros(o.shape, jnp.bool_)
        first = base = 0
        for x in group:
            inner = k - first
            row = inner % TILE - (TILE - DEPTH[x] if end else 0)
            found |= (
                (inner >= 0)
                & (inner < counts[x] * TILE)
                & (row >= 0)
                & (row < DEPTH[x])
                & (o == base + DEPTH[x] * (inner // TILE) + row)
            )
            first += counts[x] * TILE
            base += counts[x] * DEPTH[x]
        return found

    pack_rows = pack_out.shape[2]
    for g, group in enumerate(GROUPS):
        o, k = iota2(pack_rows, sum(counts[x] for x in group) * TILE)
        for end in (0, 1):
            parts = [p for x in group for p in tail_parts(x, end, range(counts[x]))]
            pack_out[g, end] = dot(
                as_bf16(travels(group, end, o, k)), jnp.concatenate(parts, axis=0)
            ).astype(BF16)
    for end in (0, 1):
        for side in (0, 1):
            parts = [
                p for x in range(6) for p in tail_parts(x, end, [counts[x] - 1 if side else 0])
            ]
            corner_out[end, side] = dot(picks[end], jnp.concatenate(parts, axis=0)).astype(BF16)
    for load in loads[10:12]:
        load.wait()
    per = spec_real.shape[1]
    spec_out[:, pl.ds(0, per)] = real_v[...].astype(BF16)
    spec_out[:, pl.ds(per, per)] = imag_v[...].astype(BF16)

    rows_of_peers = 1 + jnp.where(tm > 0, 1, 0) + jnp.where(tm < n_tm - 1, 1, 0)
    pl.semaphore_wait(barrier, n_mel * rows_of_peers - 1)
    ends = ((1, 1), (0, -1))

    def lateral(x):
        src, dst, width = inputs[x], wide[x], WIDTH[x]
        rows, cols = src.shape
        add_halo(
            0,
            1,
            src.at[:, pl.ds(cols - width, width)],
            dst.at[pl.ds(0, rows), pl.ds(EDGE - width, width)],
        )
        add_halo(
            0,
            -1,
            src.at[:, pl.ds(0, width)],
            dst.at[pl.ds(0, rows), pl.ds(EDGE + cols, width)],
        )

    for end, dt in ends:
        add_halo(dt, 0, pack_out.at[0, end], pack_in.at[0, 1 - end])
    for x in GROUPS[0]:
        lateral(x)
    for end, dt in ends:
        add_halo(dt, 1, corner_out.at[end, 1], corner_in.at[1 - end, 0])
        add_halo(dt, -1, corner_out.at[end, 0], corner_in.at[1 - end, 1])
    needed_first = len(halo)
    for end, dt in ends:
        add_halo(dt, 0, pack_out.at[1, end], pack_in.at[1, 1 - end])
    for x in GROUPS[1]:
        lateral(x)
    spec_copies = exchange(spec_out, spec_in, spec_send, spec_recv)

    for load in loads[6:10]:
        load.wait()
    w4[...] = jnp.zeros(w4.shape, BF16)
    w3[...] = jnp.zeros(w3.shape, BF16)
    half = LANES // 2
    blank = jnp.zeros((half, half), F32)
    for i in range(3):
        for k in range(4):
            lanes = pl.ds((i * 4 + k) * LANES, LANES)
            for n in range(2):
                j = n - (k - 1)
                if abs(j) <= 1:
                    w4[pl.ds(n * LANES, LANES), lanes] = k4_v[i, j + 1]
                    w3[pl.ds(n * LANES, half), lanes] = k3_v[i, j + 1]
                    w3[pl.ds(n * LANES + half, half), lanes] = k3_v[i, j + 1]
                for a in range(2):
                    pair = []
                    for b in range(2):
                        j = (2 * n + a) - (2 * (k - 1) + b)
                        pair.append(
                            k2_v[i, j + 1].astype(F32) if abs(j) <= 1 else blank
                        )
                    w2[pl.ds(n * LANES + a * half, half), lanes] = jnp.concatenate(
                        pair, axis=1
                    ).astype(BF16)
    mels = mel_power.shape[0]
    one = kernel_one[...].astype(F32)
    one = jnp.concatenate([one, one], axis=2)
    reach = 2 * (tiles - SIDE)
    row, lane = iota2(band.shape[1], LANES)
    d = row - reach - lane // half
    for i in range(3):
        value = jnp.zeros(d.shape, F32)
        for j in range(3):
            value = jnp.where(d == j - 1, one[i, j][None, :], value)
        band[i] = value
    for s in range(2, tiles - 2):
        for i in range(3):
            at = reach - 2 * (s - SIDE)
            wb[s, pl.ds(i * mels, mels)] = band[i, pl.ds(at, mels)].astype(BF16)
        wb[s, pl.ds(3 * mels, mels)] = jnp.zeros((mels, LANES), BF16)
    for g in (gb, gc):
        for s in (1, tiles - 2):
            for i in range(3):
                g[i, s] = jnp.zeros(g.shape[2:], BF16)

    loud = loudness[...]
    level = loud / (1.0 + loud * jnp.transpose(power_v[...]))
    level = jnp.concatenate([level, level], axis=1)
    lane = lax.broadcasted_iota(jnp.int32, level.shape, 1)
    gain[...] = jnp.where(lane // mels == lax.rem(mel, 2), level, 0.0)

    def tile_at(s, count=1):
        return pl.ds(pl.multiple_of(s * LANES, LANES), count * LANES)

    def prepare(s, pairs, fine_at, coarse_at, matrix):
        rows_at = pl.ds(coarse_at, matrix.shape[0])
        x = e2[pl.ds(fine_at, matrix.shape[1]), tile_at(s, 2 * pairs)]
        sums = dot(matrix, jnp.maximum(x, jnp.zeros_like(x)))
        low = lax.broadcasted_iota(jnp.int32, (matrix.shape[0], LANES), 1) < half
        for u in range(pairs):
            want = t1[rows_at, tile_at((s - SIDE) // 2 + SIDE + u)].astype(F32)
            turned = pltpu.roll(want, half, 1)
            wants = (jnp.where(low, want, turned), jnp.where(low, turned, want))
            for n in range(2):
                at = 2 * u + n
                block = sums[:, at * LANES : (at + 1) * LANES]
                pre[s + at, rows_at] = 0.25 * (block + pltpu.roll(block, half, 1) - wants[n])

    r, s_ = iota2(coarse, frames)
    pool_main = as_bf16(s_ // 2 == r, 0.25)
    r, s_ = iota2(TILE, TILE)
    pool_tail = as_bf16(coarser(s_, 0) == r, 0.25)

    def early(q, carry):
        prepare(SIDE + 8 * q, 4, 0, 0, pool_main)
        return carry

    for q in range((tiles - 2 * SIDE) // 8):
        early(q, 0)

    def arrive(g):
        for dt, dm, copy in halo[needed_first:] if g else halo[:needed_first]:
            pl.when(has(-dt, -dm))(copy.wait_recv)
        group = GROUPS[g]
        k, o = iota2(sum(counts[x] for x in group) * TILE, pack_rows)
        spots = jnp.concatenate(
            [as_bf16(travels(group, 1, o, k)), as_bf16(travels(group, 0, o, k))], axis=1
        )
        both = jnp.concatenate([pack_in[g, 0], pack_in[g, 1]], axis=0)
        placed = dot(spots, both).astype(BF16)
        first = 0
        for x in group:
            for at in range(counts[x]):
                wide[x][pl.ds(inputs[x].shape[0], TILE), pl.ds(EDGE + at * EDGE, EDGE)] = placed[
                    first : first + TILE
                ]
                first += TILE

    arrive(0)
    o, c = iota2(6 * TILE, 2 * TILE)
    spots = jnp.zeros((6 * TILE, 2 * TILE), jnp.bool_)
    for x in range(6):
        for at, base in ((0, TILE - DEPTH[x]), (1, 0)):
            r, p = o - x * TILE - base, c - at * TILE - PLACE[x]
            spots |= (r == p) & (r >= 0) & (r < DEPTH[x])
    spots = as_bf16(spots)
    for side in (0, 1):
        both = jnp.concatenate([corner_in[0, side], corner_in[1, side]], axis=0)
        placed = dot(spots, both).astype(BF16)
        for x, (src, dst) in enumerate(zip(inputs, wide)):
            at = pl.ds((counts[x] + 1) * EDGE if side else 0, EDGE)
            dst[pl.ds(src.shape[0], TILE), at] = placed[x * TILE : (x + 1) * TILE]

    def shifted(g, s, value):
        rows = value.shape[0]
        g[0, s] = pltpu.roll(value, rows - 1, 0).astype(BF16)
        g[1, s] = value.astype(BF16)
        g[2, s] = pltpu.roll(value, 1, 0).astype(BF16)

    r, s_ = iota2(coarse_rows, coarse_rows)
    mean_rows = as_bf16(r // 2 == s_ // 2, 0.25)
    r, s_ = iota2(coarse_rows, t2.shape[0])
    spread_two = as_bf16(coarser(r, coarse) == s_)

    batch = 4

    def top(b, carry):
        x = e4[:, tile_at(2 * batch * b, 2 * batch)]
        means = dot(mean_rows, jnp.maximum(x, jnp.zeros_like(x)))
        wanted = dot(spread_two, t2[:, tile_at(batch * b + SIDE // 2, batch)])
        for u in range(batch):
            one_, two = (means[:, (2 * u + n) * LANES : (2 * u + n + 1) * LANES] for n in (0, 1))
            diff = 0.25 * (one_ + two - wanted[:, u * LANES : (u + 1) * LANES])
            for n in range(2):
                at = 2 * u + n
                mask = x[:, at * LANES : (at + 1) * LANES].astype(F32) > 0
                shifted(ga, 2 * batch * b + at, jnp.where(mask, diff, 0.0))
        return carry

    for b in range(tiles // (2 * batch)):
        top(b, 0)

    arrive(1)
    for s in (2, tiles - 4):
        prepare(s, 1, 0, 0, pool_main)
    prepare(2, (tiles - 4) // 2, frames, coarse, pool_tail)

    def conv(g, weights, group, epilogue):
        rows = g.shape[2]
        pairs = (tiles - 4) // 2

        def step(q, carry):
            base = 2 + 2 * group * q
            lhs = jnp.concatenate(
                [
                    jnp.concatenate(
                        [g[i, base + 2 * u - 1 + k] for i in range(3) for k in range(4)], axis=1
                    )
                    for u in range(group)
                ],
                axis=0,
            )
            result = dot_nt(lhs, weights[...])
            for u in range(group):
                epilogue(base + 2 * u, result[u * rows : (u + 1) * rows])
            return carry

        for q in range(pairs // group):
            step(q, 0)

    def third(s, value):
        x = e3[:, tile_at(s, 2)].astype(F32)
        masked = jnp.where(x > 0, value, 0.0)
        for n in range(2):
            shifted(gb, s + n, masked[:, n * LANES : (n + 1) * LANES])

    conv(ga, w4, 6, third)

    r, s_ = iota2(fine_rows, coarse_rows)
    spread_rows = as_bf16(coarser(r, frames) == s_)

    def second(s, value):
        x = e2[:, tile_at(s, 2)].astype(F32)
        parts = []
        for n in range(2):
            lanes = slice(n * LANES, (n + 1) * LANES)
            parts.append((0.25 * value[:, lanes] + pre[s + n]).astype(BF16))
        fine = dot(spread_rows, jnp.concatenate(parts, axis=1))
        masked = jnp.where(x > 0, fine, 0.0)
        for n in range(2):
            shifted(gc, s + n, masked[:, n * LANES : (n + 1) * LANES])

    conv(gb, w3, 6, second)

    def first(s, value):
        x = e1[:, tile_at(s, 2)].astype(F32)
        masked = jnp.where(x > 0, value, 0.0).astype(BF16)
        for n in range(2):
            gd[s + n] = masked[:, n * LANES : (n + 1) * LANES]

    conv(gc, w2, 3, first)

    total = jnp.zeros((fine_rows, 4 * mels), F32)
    span = 12
    for s in range(2, tiles - 2, span):
        total += dot_nt(
            jnp.concatenate([gd[s + k] for k in range(span)], axis=1),
            jnp.concatenate([wb[s + k] for k in range(span)], axis=1),
        )
    left, right = total[:, : 2 * mels], total[:, 2 * mels :]
    grad_log = (
        pltpu.roll(left, fine_rows - 1, 0) + pltpu.roll(left, mels, 1) + pltpu.roll(right, 1, 0)
    )[:frames, :mels]
    mel_out[...] = (jnp.concatenate([grad_log, grad_log], axis=1) * gain[...]).astype(BF16)
    mel_copies = exchange(mel_out, mel_in, mel_send, mel_recv)

    for dt, dm, copy in halo:
        pl.when(has(dt, dm))(copy.wait_send)
    loads[12].wait()
    filters_b[...] = filters_v[...].astype(BF16)
    finish(spec_copies)
    loads[13].wait()
    finish(mel_copies)

    whole = jnp.concatenate(
        [mel_in[2 * a] + mel_in[2 * a + 1] for a in range(n_mel // 2)], axis=1
    )
    power = dot_nt(whole, filters_b[...])
    grads = []
    for part in range(2):
        for j in range(n_mel):
            spec = spec_in[j, :, pl.ds(part * per, per)].astype(F32)
            grads.append((power[:, j * per : (j + 1) * per] * spec).astype(BF16))
    made = dot(jnp.concatenate(grads, axis=1), table_v[...])
    hop = made.shape[1] // 2
    blocks = made[:, :hop] + pltpu.roll(made[:, hop:], 1, 0)
    for a in range(hop // LANES):
        out[pl.ds(a, share, stride=hop // LANES), :] = blocks[
            :share, a * LANES : (a + 1) * LANES
        ]


def shards(
    act_one,
    act_two,
    act_three,
    act_four,
    target_one,
    target_two,
    kernel_one,
    kernel_two,
    kernel_three,
    kernel_four,
    mel_power,
    loudness,
    filters,
    spec_real,
    spec_imag,
):
    n_tm, n_mel = lax.axis_size("tm"), lax.axis_size("mel")
    frames, mels = mel_power.shape
    bins = filters.shape[0]
    table = jnp.asarray(synthesis_table(bins))
    share = frames // n_mel
    ext = lambda a: pltpu.VMEM((a.shape[0] + TILE, a.shape[1] + 2 * EDGE), BF16)
    length = act_one.shape[1]
    tiles = (length + 2 * EDGE) // LANES
    fine_rows, coarse_rows = frames + TILE, frames // 2 + TILE
    arrays = (act_one, act_two, act_three, act_four, target_one, target_two)
    pack_rows = max(
        sum(DEPTH[x] * (arrays[x].shape[1] // EDGE) for x in group) for group in GROUPS
    )
    pack_rows = -(-pack_rows // TILE) * TILE
    any_spec = pl.BlockSpec(memory_space=pl.ANY)
    vmem = pl.BlockSpec(memory_space=pltpu.VMEM)
    result = pl.pallas_call(
        functools.partial(kernel, n_tm, n_mel),
        out_shape=jax.ShapeDtypeStruct((share * bins // LANES, LANES), F32),
        in_specs=[any_spec] * 8 + [vmem] + [any_spec] * 4 + [vmem] + [any_spec] * 2,
        out_specs=vmem,
        scratch_shapes=[
            ext(act_one),
            ext(act_two),
            ext(act_three),
            ext(act_four),
            ext(target_one),
            ext(target_two),
            pltpu.VMEM(filters.shape, F32),
            pltpu.VMEM(table.shape, BF16),
            pltpu.VMEM((2, 2, pack_rows, EDGE), BF16),
            pltpu.VMEM((2, 2, pack_rows, EDGE), BF16),
            pltpu.VMEM((2, 2, TILE, EDGE), BF16),
            pltpu.VMEM((2, 2, TILE, EDGE), BF16),
            pltpu.VMEM((3, tiles, coarse_rows, LANES), BF16),
            pltpu.VMEM((3, tiles, coarse_rows, LANES), BF16),
            pltpu.VMEM((3, tiles, fine_rows, LANES), BF16),
            pltpu.VMEM((tiles, fine_rows, LANES), BF16),
            pltpu.VMEM((tiles, coarse_rows, LANES), F32),
            pltpu.VMEM((frames, 2 * mels), F32),
            pltpu.VMEM(filters.shape, BF16),
            pltpu.VMEM(kernel_two.shape, BF16),
            pltpu.VMEM(kernel_three.shape, BF16),
            pltpu.VMEM(kernel_four.shape, BF16),
            pltpu.VMEM((mels, frames), F32),
            pltpu.VMEM(spec_real.shape, F32),
            pltpu.VMEM(spec_imag.shape, F32),
            pltpu.VMEM((2 * LANES, 12 * LANES), BF16),
            pltpu.VMEM((2 * LANES, 12 * LANES), BF16),
            pltpu.VMEM((2 * LANES, 12 * LANES), BF16),
            pltpu.VMEM((3, 2 * (tiles + SIDE) + mels, LANES), F32),
            pltpu.VMEM((tiles, 4 * mels, LANES), BF16),
            pltpu.VMEM((frames, 2 * spec_real.shape[1]), BF16),
            pltpu.VMEM((n_mel, share + TILE, 2 * spec_real.shape[1]), BF16),
            pltpu.VMEM((frames, 2 * mels), BF16),
            pltpu.VMEM((n_mel, share + TILE, 2 * mels), BF16),
            pltpu.SemaphoreType.DMA((14,)),
            pltpu.SemaphoreType.DMA((20,)),
            pltpu.SemaphoreType.DMA((20,)),
            pltpu.SemaphoreType.DMA((2 * n_mel,)),
            pltpu.SemaphoreType.DMA((2 * n_mel,)),
            pltpu.SemaphoreType.DMA((2 * n_mel,)),
            pltpu.SemaphoreType.DMA((2 * n_mel,)),
        ],
        compiler_params=pltpu.CompilerParams(
            collective_id=0, has_side_effects=True, vmem_limit_bytes=56 * 2**20
        ),
        name="wave_gradient",
    )(
        act_one,
        act_two,
        act_three,
        act_four,
        target_one,
        target_two,
        filters,
        table,
        jnp.transpose(kernel_one, (0, 2, 1, 3)).reshape(3, 3, kernel_one.shape[3]),
        kernel_two,
        kernel_three,
        kernel_four,
        mel_power.T,
        loudness.reshape(1, mels),
        spec_real,
        spec_imag,
    )
    return result.reshape(-1)


def solution(mesh):
    return jax.shard_map(
        shards,
        mesh=mesh,
        in_specs=(
            P("tm", "mel"),
            P("tm", "mel"),
            P("tm", "mel"),
            P("tm", "mel"),
            P("tm", "mel"),
            P("tm", "mel"),
            P(),
            P(),
            P(),
            P(),
            P("tm", "mel"),
            P("mel"),
            P(),
            P("tm", "mel"),
            P("tm", "mel"),
        ),
        out_specs=P(("tm", "mel")),
        check_vma=False,
    )
```

```python
import functools

import jax
import jax.numpy as jnp
import ml_dtypes
import numpy as np
from jax import lax
from jax.experimental import pallas as pl
from jax.experimental.pallas import tpu as pltpu
from jax.sharding import PartitionSpec as P

LANES = 128
TILE = 16
SIDE = 4
EDGE = SIDE * LANES
MESH = pl.DeviceIdType.MESH
BF16 = jnp.bfloat16
F32 = jnp.float32

DEPTH = (1, 2, 2, 4, 1, 2)
PLACE = (0, 1, 3, 5, 9, 10)
WIDTH = (128, 128, 256, 512, 128, 256)
GROUPS = ((3, 5), (2, 1, 0, 4))


def synthesis_table(bins):
    points, hop = 2 * bins, bins
    bin_at = np.concatenate([np.arange(0, bins, 2), np.arange(1, bins, 2)])
    angle = (bin_at[:, None] * np.arange(hop)[None, :] % points) * (2.0 * np.pi / points)
    scale = 2.0 * points**-0.5
    half = bins // 2
    parts = []
    for at in (slice(0, half), slice(half, bins)):
        parts += [np.cos(angle[at]) * scale, -np.sin(angle[at]) * scale]
    return np.concatenate(parts, axis=0).astype(np.float32).astype(ml_dtypes.bfloat16)


def hann_halves(bins):
    points = 2 * bins
    window = 0.5 - 0.5 * np.cos(np.arange(points) * (2.0 * np.pi / points))
    return window.reshape(2, bins).astype(np.float32)


def iota2(rows, cols):
    return (
        lax.broadcasted_iota(jnp.int32, (rows, cols), 0),
        lax.broadcasted_iota(jnp.int32, (rows, cols), 1),
    )


def as_bf16(mask, value=1.0):
    return jnp.where(mask, value, 0.0).astype(F32).astype(BF16)


def coarser(row, main):
    return row // 2 + jnp.where(row >= main + TILE // 2, TILE // 2, 0)


def dot(a, b):
    return jnp.dot(a, b, preferred_element_type=F32)


def dot_nt(a, b):
    return lax.dot_general(a, b, (((1,), (1,)), ((), ())), preferred_element_type=F32)


def kernel(
    n_tm,
    n_mel,
    act_one,
    act_two,
    act_three,
    act_four,
    target_one,
    target_two,
    filters,
    table,
    kernel_one,
    kernel_two,
    kernel_three,
    kernel_four,
    mel_power,
    loudness,
    spec_real,
    spec_imag,
    window,
    out,
    e1,
    e2,
    e3,
    e4,
    t1,
    t2,
    filters_v,
    table_v,
    pack_out,
    pack_in,
    corner_out,
    corner_in,
    ga,
    gb,
    gc,
    gd,
    pre,
    gain,
    filters_b,
    k2_v,
    k3_v,
    k4_v,
    power_v,
    real_v,
    imag_v,
    w4,
    w3,
    w2,
    band,
    wb,
    spec_out,
    spec_in,
    mel_out,
    mel_in,
    load_sem,
    halo_send,
    halo_recv,
    spec_send,
    spec_recv,
    mel_send,
    mel_recv,
):
    tm, mel = lax.axis_index("tm"), lax.axis_index("mel")
    length = act_one.shape[1]
    inputs = (act_one, act_two, act_three, act_four, target_one, target_two)
    wide = (e1, e2, e3, e4, t1, t2)
    frames, coarse = act_one.shape[0], act_three.shape[0]
    fine_rows, coarse_rows = e1.shape[0], e3.shape[0]
    tiles = e1.shape[1] // LANES
    share = frames // n_mel

    loads = []
    for at, (src, dst) in enumerate(zip(inputs, wide)):
        rows, cols = src.shape
        loads.append(
            pltpu.make_async_copy(
                src, dst.at[pl.ds(0, rows), pl.ds(EDGE, cols)], load_sem.at[at]
            )
        )
    for src, dst in (
        (kernel_two, k2_v),
        (kernel_three, k3_v),
        (kernel_four, k4_v),
        (mel_power, power_v),
        (spec_real, real_v),
        (spec_imag, imag_v),
        (filters.at[:, pl.ds(0, LANES)], filters_v.at[0]),
        (filters.at[:, pl.ds(LANES, LANES)], filters_v.at[1]),
        (table, table_v),
    ):
        loads.append(pltpu.make_async_copy(src, dst, load_sem.at[len(loads)]))
    for load in loads:
        load.start()

    for src, dst in zip(inputs, wide):
        rows, cols = src.shape
        dst[pl.ds(0, rows), pl.ds(0, EDGE)] = jnp.zeros((rows, EDGE), BF16)
        dst[pl.ds(0, rows), pl.ds(EDGE + cols, EDGE)] = jnp.zeros((rows, EDGE), BF16)
    pack_in[...] = jnp.zeros(pack_in.shape, BF16)
    corner_in[...] = jnp.zeros(corner_in.shape, BF16)
    spec_in[...] = jnp.zeros(spec_in.shape, BF16)
    mel_in[...] = jnp.zeros(mel_in.shape, BF16)

    barrier = pltpu.get_barrier_semaphore()

    def has(dt, dm):
        cond = jnp.bool_(True)
        if dt:
            cond = (tm > 0) if dt < 0 else (tm < n_tm - 1)
        if dm:
            side = (mel > 0) if dm < 0 else (mel < n_mel - 1)
            cond = side if not dt else jnp.logical_and(cond, side)
        return cond

    for dt in (-1, 0, 1):
        for k in range(n_mel):
            if dt == 0 and k == 0:
                continue

            def greet(dt=dt, k=k):
                pl.semaphore_signal(
                    barrier,
                    inc=1,
                    device_id={"tm": tm + dt, "mel": lax.rem(mel + k, n_mel)},
                    device_id_type=MESH,
                )

            if dt:
                pl.when(has(dt, 0))(greet)
            else:
                greet()

    halo = []

    def add_halo(dt, dm, src, dst):
        at = len(halo)
        copy = pltpu.make_async_remote_copy(
            src_ref=src,
            dst_ref=dst,
            send_sem=halo_send.at[at],
            recv_sem=halo_recv.at[at],
            device_id={"tm": tm + dt, "mel": mel + dm},
            device_id_type=MESH,
        )
        halo.append((dt, dm, copy))
        pl.when(has(dt, dm))(copy.start)

    def exchange(src, dst, send, recv):
        copies = []
        for k in range(n_mel):
            j = lax.rem(mel + k, n_mel)
            main = pl.ds(pl.multiple_of(j * share, TILE), share)
            before = pl.ds(
                pl.multiple_of(lax.rem(j * share + frames - TILE, frames), TILE), TILE
            )
            if k:
                copy = pltpu.make_async_remote_copy(
                    src_ref=src.at[main],
                    dst_ref=dst.at[mel, pl.ds(0, share)],
                    send_sem=send.at[k],
                    recv_sem=recv.at[k],
                    device_id={"tm": tm, "mel": j},
                    device_id_type=MESH,
                )
                copy.start()
                copies.append((copy, None, None))
            copy = pltpu.make_async_remote_copy(
                src_ref=src.at[before],
                dst_ref=dst.at[mel, pl.ds(share, TILE)],
                send_sem=send.at[n_mel + k],
                recv_sem=recv.at[n_mel + k],
                device_id={"tm": tm + jnp.where(j == 0, 1, 0), "mel": j},
                device_id_type=MESH,
            )
            if k:
                sends = jnp.logical_or(j > 0, tm < n_tm - 1)
                receives = jnp.logical_or(mel > 0, tm > 0)
            else:
                sends = jnp.logical_and(mel == 0, tm < n_tm - 1)
                receives = jnp.logical_and(mel == 0, tm > 0)
            pl.when(sends)(copy.start)
            copies.append((copy, sends, receives))
        dst[mel, pl.ds(0, share)] = src[pl.ds(pl.multiple_of(mel * share, TILE), share)]

        @pl.when(mel > 0)
        def _():
            dst[mel, pl.ds(share, TILE)] = src[
                pl.ds(pl.multiple_of(mel * share - TILE, TILE), TILE)
            ]

        return copies

    def finish(copies):
        for copy, sends, receives in copies:
            if sends is None:
                copy.wait_recv()
            else:
                pl.when(receives)(copy.wait_recv)
        for copy, sends, receives in copies:
            if sends is None:
                copy.wait_send()
            else:
                pl.when(sends)(copy.wait_send)

    for load in loads[:6]:
        load.wait()
    o, c = iota2(TILE, 6 * TILE)
    first_rows = jnp.zeros((TILE, 6 * TILE), jnp.bool_)
    last_rows = jnp.zeros((TILE, 6 * TILE), jnp.bool_)
    for x in range(6):
        inside = (o >= PLACE[x]) & (o < PLACE[x] + DEPTH[x])
        first_rows |= inside & (c - x * TILE == o - PLACE[x])
        last_rows |= inside & (c - x * TILE - (TILE - DEPTH[x]) == o - PLACE[x])
    picks = (as_bf16(first_rows), as_bf16(last_rows))
    counts = [src.shape[1] // EDGE for src in inputs]

    def tail_parts(x, end, chunks):
        src, dst = inputs[x], wide[x]
        row = src.shape[0] - TILE if end else 0
        return [dst[pl.ds(row, TILE), pl.ds(EDGE + at * EDGE, EDGE)] for at in chunks]

    def travels(group, end, o, k):
        found = jnp.zeros(o.shape, jnp.bool_)
        first = base = 0
        for x in group:
            inner = k - first
            row = inner % TILE - (TILE - DEPTH[x] if end else 0)
            found |= (
                (inner >= 0)
                & (inner < counts[x] * TILE)
                & (row >= 0)
                & (row < DEPTH[x])
                & (o == base + DEPTH[x] * (inner // TILE) + row)
            )
            first += counts[x] * TILE
            base += counts[x] * DEPTH[x]
        return found

    pack_rows = pack_out.shape[2]
    for g, group in enumerate(GROUPS):
        o, k = iota2(pack_rows, sum(counts[x] for x in group) * TILE)
        for end in (0, 1):
            parts = [p for x in group for p in tail_parts(x, end, range(counts[x]))]
            pack_out[g, end] = dot(
                as_bf16(travels(group, end, o, k)), jnp.concatenate(parts, axis=0)
            ).astype(BF16)
    for end in (0, 1):
        for side in (0, 1):
            parts = [
                p for x in range(6) for p in tail_parts(x, end, [counts[x] - 1 if side else 0])
            ]
            corner_out[end, side] = dot(picks[end], jnp.concatenate(parts, axis=0)).astype(BF16)
    for load in loads[10:12]:
        load.wait()
    per = spec_real.shape[1]
    k, c = iota2(per, per)
    even_first = as_bf16(k == jnp.where(c < per // 2, 2 * c, 2 * c - per + 1))
    spec_out[:, pl.ds(0, per)] = dot(real_v[...].astype(BF16), even_first).astype(BF16)
    spec_out[:, pl.ds(per, per)] = dot(imag_v[...].astype(BF16), even_first).astype(BF16)

    rows_of_peers = 1 + jnp.where(tm > 0, 1, 0) + jnp.where(tm < n_tm - 1, 1, 0)
    pl.semaphore_wait(barrier, n_mel * rows_of_peers - 1)
    ends = ((1, 1), (0, -1))

    def lateral(x):
        src, dst, width = inputs[x], wide[x], WIDTH[x]
        rows, cols = src.shape
        add_halo(
            0,
            1,
            src.at[:, pl.ds(cols - width, width)],
            dst.at[pl.ds(0, rows), pl.ds(EDGE - width, width)],
        )
        add_halo(
            0,
            -1,
            src.at[:, pl.ds(0, width)],
            dst.at[pl.ds(0, rows), pl.ds(EDGE + cols, width)],
        )

    for end, dt in ends:
        add_halo(dt, 0, pack_out.at[0, end], pack_in.at[0, 1 - end])
    for x in GROUPS[0]:
        lateral(x)
    for end, dt in ends:
        add_halo(dt, 1, corner_out.at[end, 1], corner_in.at[1 - end, 0])
        add_halo(dt, -1, corner_out.at[end, 0], corner_in.at[1 - end, 1])
    needed_first = len(halo)
    for end, dt in ends:
        add_halo(dt, 0, pack_out.at[1, end], pack_in.at[1, 1 - end])
    for x in GROUPS[1]:
        lateral(x)
    spec_copies = exchange(spec_out, spec_in, spec_send, spec_recv)

    for load in loads[6:10]:
        load.wait()
    w4[...] = jnp.zeros(w4.shape, BF16)
    w3[...] = jnp.zeros(w3.shape, BF16)
    half = LANES // 2
    blank = jnp.zeros((half, half), F32)
    for i in range(3):
        for k in range(4):
            lanes = pl.ds((i * 4 + k) * LANES, LANES)
            for n in range(2):
                j = n - (k - 1)
                if abs(j) <= 1:
                    w4[pl.ds(n * LANES, LANES), lanes] = k4_v[i, j + 1]
                    w3[pl.ds(n * LANES, half), lanes] = k3_v[i, j + 1]
                    w3[pl.ds(n * LANES + half, half), lanes] = k3_v[i, j + 1]
                for a in range(2):
                    pair = []
                    for b in range(2):
                        j = (2 * n + a) - (2 * (k - 1) + b)
                        pair.append(
                            k2_v[i, j + 1].astype(F32) if abs(j) <= 1 else blank
                        )
                    w2[pl.ds(n * LANES + a * half, half), lanes] = jnp.concatenate(
                        pair, axis=1
                    ).astype(BF16)
    mels = mel_power.shape[0]
    one = kernel_one[...].astype(F32)
    one = jnp.concatenate([one, one], axis=2)
    reach = 2 * (tiles - SIDE)
    row, lane = iota2(band.shape[1], LANES)
    d = row - reach - lane // half
    for i in range(3):
        value = jnp.zeros(d.shape, F32)
        for j in range(3):
            value = jnp.where(d == j - 1, one[i, j][None, :], value)
        band[i] = value
    for s in range(2, tiles - 2):
        for i in range(3):
            at = reach - 2 * (s - SIDE)
            wb[s, pl.ds(i * mels, mels)] = band[i, pl.ds(at, mels)].astype(BF16)
        wb[s, pl.ds(3 * mels, mels)] = jnp.zeros((mels, LANES), BF16)
    for g in (gb, gc):
        for s in (1, tiles - 2):
            for i in range(3):
                g[i, s] = jnp.zeros(g.shape[2:], BF16)

    loud = loudness[...]
    level = loud / (1.0 + loud * jnp.transpose(power_v[...]))
    level = jnp.concatenate([level, level], axis=1)
    lane = lax.broadcasted_iota(jnp.int32, level.shape, 1)
    gain[...] = jnp.where(lane // mels == lax.rem(mel, 2), level, 0.0)

    def tile_at(s, count=1):
        return pl.ds(pl.multiple_of(s * LANES, LANES), count * LANES)

    def prepare(s, pairs, fine_at, coarse_at, matrix):
        rows_at = pl.ds(coarse_at, matrix.shape[0])
        x = e2[pl.ds(fine_at, matrix.shape[1]), tile_at(s, 2 * pairs)]
        sums = dot(matrix, jnp.maximum(x, jnp.zeros_like(x)))
        low = lax.broadcasted_iota(jnp.int32, (matrix.shape[0], LANES), 1) < half
        for u in range(pairs):
            want = t1[rows_at, tile_at((s - SIDE) // 2 + SIDE + u)].astype(F32)
            turned = pltpu.roll(want, half, 1)
            wants = (jnp.where(low, want, turned), jnp.where(low, turned, want))
            for n in range(2):
                at = 2 * u + n
                block = sums[:, at * LANES : (at + 1) * LANES]
                pre[s + at, rows_at] = 0.25 * (block + pltpu.roll(block, half, 1) - wants[n])

    r, s_ = iota2(coarse, frames)
    pool_main = as_bf16(s_ // 2 == r, 0.25)
    r, s_ = iota2(TILE, TILE)
    pool_tail = as_bf16(coarser(s_, 0) == r, 0.25)

    def early(q, carry):
        prepare(SIDE + 8 * q, 4, 0, 0, pool_main)
        return carry

    for q in range((tiles - 2 * SIDE) // 8):
        early(q, 0)

    def arrive(g):
        for dt, dm, copy in halo[needed_first:] if g else halo[:needed_first]:
            pl.when(has(-dt, -dm))(copy.wait_recv)
        group = GROUPS[g]
        k, o = iota2(sum(counts[x] for x in group) * TILE, pack_rows)
        spots = jnp.concatenate(
            [as_bf16(travels(group, 1, o, k)), as_bf16(travels(group, 0, o, k))], axis=1
        )
        both = jnp.concatenate([pack_in[g, 0], pack_in[g, 1]], axis=0)
        placed = dot(spots, both).astype(BF16)
        first = 0
        for x in group:
            for at in range(counts[x]):
                wide[x][pl.ds(inputs[x].shape[0], TILE), pl.ds(EDGE + at * EDGE, EDGE)] = placed[
                    first : first + TILE
                ]
                first += TILE

    arrive(0)
    o, c = iota2(6 * TILE, 2 * TILE)
    spots = jnp.zeros((6 * TILE, 2 * TILE), jnp.bool_)
    for x in range(6):
        for at, base in ((0, TILE - DEPTH[x]), (1, 0)):
            r, p = o - x * TILE - base, c - at * TILE - PLACE[x]
            spots |= (r == p) & (r >= 0) & (r < DEPTH[x])
    spots = as_bf16(spots)
    for side in (0, 1):
        both = jnp.concatenate([corner_in[0, side], corner_in[1, side]], axis=0)
        placed = dot(spots, both).astype(BF16)
        for x, (src, dst) in enumerate(zip(inputs, wide)):
            at = pl.ds((counts[x] + 1) * EDGE if side else 0, EDGE)
            dst[pl.ds(src.shape[0], TILE), at] = placed[x * TILE : (x + 1) * TILE]

    def shifted(g, s, value):
        rows = value.shape[0]
        g[0, s] = pltpu.roll(value, rows - 1, 0).astype(BF16)
        g[1, s] = value.astype(BF16)
        g[2, s] = pltpu.roll(value, 1, 0).astype(BF16)

    r, s_ = iota2(coarse_rows, coarse_rows)
    mean_rows = as_bf16(r // 2 == s_ // 2, 0.25)
    r, s_ = iota2(coarse_rows, t2.shape[0])
    spread_two = as_bf16(coarser(r, coarse) == s_)

    batch = 4

    def top(b, carry):
        x = e4[:, tile_at(2 * batch * b, 2 * batch)]
        means = dot(mean_rows, jnp.maximum(x, jnp.zeros_like(x)))
        wanted = dot(spread_two, t2[:, tile_at(batch * b + SIDE // 2, batch)])
        for u in range(batch):
            one_, two = (means[:, (2 * u + n) * LANES : (2 * u + n + 1) * LANES] for n in (0, 1))
            diff = 0.25 * (one_ + two - wanted[:, u * LANES : (u + 1) * LANES])
            for n in range(2):
                at = 2 * u + n
                mask = x[:, at * LANES : (at + 1) * LANES].astype(F32) > 0
                shifted(ga, 2 * batch * b + at, jnp.where(mask, diff, 0.0))
        return carry

    for b in range(tiles // (2 * batch)):
        top(b, 0)

    arrive(1)
    for s in (2, tiles - 4):
        prepare(s, 1, 0, 0, pool_main)
    prepare(2, (tiles - 4) // 2, frames, coarse, pool_tail)

    def conv(g, weights, group, epilogue):
        rows = g.shape[2]
        pairs = (tiles - 4) // 2

        def step(q, carry):
            base = 2 + 2 * group * q
            lhs = jnp.concatenate(
                [
                    jnp.concatenate(
                        [g[i, base + 2 * u - 1 + k] for i in range(3) for k in range(4)], axis=1
                    )
                    for u in range(group)
                ],
                axis=0,
            )
            result = dot_nt(lhs, weights[...])
            for u in range(group):
                epilogue(base + 2 * u, result[u * rows : (u + 1) * rows])
            return carry

        for q in range(pairs // group):
            step(q, 0)

    def third(s, value):
        x = e3[:, tile_at(s, 2)].astype(F32)
        masked = jnp.where(x > 0, value, 0.0)
        for n in range(2):
            shifted(gb, s + n, masked[:, n * LANES : (n + 1) * LANES])

    conv(ga, w4, 6, third)

    r, s_ = iota2(fine_rows, coarse_rows)
    spread_rows = as_bf16(coarser(r, frames) == s_)

    def second(s, value):
        x = e2[:, tile_at(s, 2)].astype(F32)
        parts = []
        for n in range(2):
            lanes = slice(n * LANES, (n + 1) * LANES)
            parts.append((0.25 * value[:, lanes] + pre[s + n]).astype(BF16))
        fine = dot(spread_rows, jnp.concatenate(parts, axis=1))
        masked = jnp.where(x > 0, fine, 0.0)
        for n in range(2):
            shifted(gc, s + n, masked[:, n * LANES : (n + 1) * LANES])

    conv(gb, w3, 6, second)

    def first(s, value):
        x = e1[:, tile_at(s, 2)].astype(F32)
        masked = jnp.where(x > 0, value, 0.0).astype(BF16)
        for n in range(2):
            gd[s + n] = masked[:, n * LANES : (n + 1) * LANES]

    conv(gc, w2, 3, first)

    total = jnp.zeros((fine_rows, 4 * mels), F32)
    span = 12
    for s in range(2, tiles - 2, span):
        total += dot_nt(
            jnp.concatenate([gd[s + k] for k in range(span)], axis=1),
            jnp.concatenate([wb[s + k] for k in range(span)], axis=1),
        )
    left, right = total[:, : 2 * mels], total[:, 2 * mels :]
    grad_log = (
        pltpu.roll(left, fine_rows - 1, 0) + pltpu.roll(left, mels, 1) + pltpu.roll(right, 1, 0)
    )[:frames, :mels]
    mel_out[...] = (jnp.concatenate([grad_log, grad_log], axis=1) * gain[...]).astype(BF16)
    mel_copies = exchange(mel_out, mel_in, mel_send, mel_recv)

    for dt, dm, copy in halo:
        pl.when(has(dt, dm))(copy.wait_send)
    loads[12].wait()
    loads[13].wait()
    bins = filters.shape[0]
    for a in range(2):
        for odd in (0, 1):
            filters_b[pl.ds(odd * (bins // 2), bins // 2), pl.ds(a * LANES, LANES)] = filters_v[
                a, pl.ds(odd, bins // 2, stride=2), :
            ].astype(BF16)
    finish(spec_copies)
    low = lax.broadcasted_iota(jnp.int32, (spec_in.shape[1], per), 1) < per // 2
    specs = ([], [])
    for part in range(2):
        for a in range(n_mel // 2):
            one_, two = (
                spec_in[2 * a + b, :, pl.ds(part * per, per)].astype(F32) for b in (0, 1)
            )
            specs[0].append(jnp.where(low, one_, pltpu.roll(two, per // 2, 1)))
            specs[1].append(jnp.where(low, pltpu.roll(one_, per // 2, 1), two))
    specs = [jnp.concatenate(parts, axis=1) for parts in specs]
    loads[14].wait()
    finish(mel_copies)

    whole = jnp.concatenate(
        [mel_in[2 * a] + mel_in[2 * a + 1] for a in range(n_mel // 2)], axis=1
    )
    power = dot_nt(whole, filters_b[...])
    made = []
    for odd in (0, 1):
        level = power[:, odd * (bins // 2) : (odd + 1) * (bins // 2)]
        grads = (jnp.concatenate([level, level], axis=1) * specs[odd]).astype(BF16)
        made.append(dot(grads, table_v[pl.ds(odd * bins, bins), :]))
    hop = made[0].shape[1]
    halves = window[...]
    blocks = (made[0] + made[1]) * halves[0:1] + pltpu.roll(
        (made[0] - made[1]) * halves[1:2], 1, 0
    )
    for a in range(hop // LANES):
        out[pl.ds(a, share, stride=hop // LANES), :] = blocks[
            :share, a * LANES : (a + 1) * LANES
        ]


def shards(
    act_one,
    act_two,
    act_three,
    act_four,
    target_one,
    target_two,
    kernel_one,
    kernel_two,
    kernel_three,
    kernel_four,
    mel_power,
    loudness,
    filters,
    spec_real,
    spec_imag,
):
    n_tm, n_mel = lax.axis_size("tm"), lax.axis_size("mel")
    frames, mels = mel_power.shape
    bins = filters.shape[0]
    table = jnp.asarray(synthesis_table(bins))
    share = frames // n_mel
    ext = lambda a: pltpu.VMEM((a.shape[0] + TILE, a.shape[1] + 2 * EDGE), BF16)
    length = act_one.shape[1]
    tiles = (length + 2 * EDGE) // LANES
    fine_rows, coarse_rows = frames + TILE, frames // 2 + TILE
    arrays = (act_one, act_two, act_three, act_four, target_one, target_two)
    pack_rows = max(
        sum(DEPTH[x] * (arrays[x].shape[1] // EDGE) for x in group) for group in GROUPS
    )
    pack_rows = -(-pack_rows // TILE) * TILE
    any_spec = pl.BlockSpec(memory_space=pl.ANY)
    vmem = pl.BlockSpec(memory_space=pltpu.VMEM)
    result = pl.pallas_call(
        functools.partial(kernel, n_tm, n_mel),
        out_shape=jax.ShapeDtypeStruct((share * bins // LANES, LANES), F32),
        in_specs=[any_spec] * 8 + [vmem] + [any_spec] * 4 + [vmem] + [any_spec] * 2 + [vmem],
        out_specs=vmem,
        scratch_shapes=[
            ext(act_one),
            ext(act_two),
            ext(act_three),
            ext(act_four),
            ext(target_one),
            ext(target_two),
            pltpu.VMEM((2, bins, LANES), F32),
            pltpu.VMEM(table.shape, BF16),
            pltpu.VMEM((2, 2, pack_rows, EDGE), BF16),
            pltpu.VMEM((2, 2, pack_rows, EDGE), BF16),
            pltpu.VMEM((2, 2, TILE, EDGE), BF16),
            pltpu.VMEM((2, 2, TILE, EDGE), BF16),
            pltpu.VMEM((3, tiles, coarse_rows, LANES), BF16),
            pltpu.VMEM((3, tiles, coarse_rows, LANES), BF16),
            pltpu.VMEM((3, tiles, fine_rows, LANES), BF16),
            pltpu.VMEM((tiles, fine_rows, LANES), BF16),
            pltpu.VMEM((tiles, coarse_rows, LANES), F32),
            pltpu.VMEM((frames, 2 * mels), F32),
            pltpu.VMEM(filters.shape, BF16),
            pltpu.VMEM(kernel_two.shape, BF16),
            pltpu.VMEM(kernel_three.shape, BF16),
            pltpu.VMEM(kernel_four.shape, BF16),
            pltpu.VMEM((mels, frames), F32),
            pltpu.VMEM(spec_real.shape, F32),
            pltpu.VMEM(spec_imag.shape, F32),
            pltpu.VMEM((2 * LANES, 12 * LANES), BF16),
            pltpu.VMEM((2 * LANES, 12 * LANES), BF16),
            pltpu.VMEM((2 * LANES, 12 * LANES), BF16),
            pltpu.VMEM((3, 2 * (tiles + SIDE) + mels, LANES), F32),
            pltpu.VMEM((tiles, 4 * mels, LANES), BF16),
            pltpu.VMEM((frames, 2 * spec_real.shape[1]), BF16),
            pltpu.VMEM((n_mel, share + TILE, 2 * spec_real.shape[1]), BF16),
            pltpu.VMEM((frames, 2 * mels), BF16),
            pltpu.VMEM((n_mel, share + TILE, 2 * mels), BF16),
            pltpu.SemaphoreType.DMA((15,)),
            pltpu.SemaphoreType.DMA((20,)),
            pltpu.SemaphoreType.DMA((20,)),
            pltpu.SemaphoreType.DMA((2 * n_mel,)),
            pltpu.SemaphoreType.DMA((2 * n_mel,)),
            pltpu.SemaphoreType.DMA((2 * n_mel,)),
            pltpu.SemaphoreType.DMA((2 * n_mel,)),
        ],
        compiler_params=pltpu.CompilerParams(
            collective_id=0, has_side_effects=True, vmem_limit_bytes=56 * 2**20
        ),
        name="wave_gradient",
    )(
        act_one,
        act_two,
        act_three,
        act_four,
        target_one,
        target_two,
        filters,
        table,
        jnp.transpose(kernel_one, (0, 2, 1, 3)).reshape(3, 3, kernel_one.shape[3]),
        kernel_two,
        kernel_three,
        kernel_four,
        mel_power.T,
        loudness.reshape(1, mels),
        spec_real,
        spec_imag,
        jnp.asarray(hann_halves(bins)),
    )
    return result.reshape(-1)


def solution(mesh):
    return jax.shard_map(
        shards,
        mesh=mesh,
        in_specs=(
            P("tm", "mel"),
            P("tm", "mel"),
            P("tm", "mel"),
            P("tm", "mel"),
            P("tm", "mel"),
            P("tm", "mel"),
            P(),
            P(),
            P(),
            P(),
            P("tm", "mel"),
            P("mel"),
            P(),
            P("tm", "mel"),
            P("tm", "mel"),
        ),
        out_specs=P(("tm", "mel")),
        check_vma=False,
    )
```

```python
import functools

import jax
import jax.numpy as jnp
import ml_dtypes
import numpy as np
from jax import lax
from jax.experimental import pallas as pl
from jax.experimental.pallas import tpu as pltpu
from jax.sharding import PartitionSpec as P

LANES = 128
TILE = 16
SIDE = 4
EDGE = SIDE * LANES
MESH = pl.DeviceIdType.MESH
BF16 = jnp.bfloat16
F32 = jnp.float32

DEPTH = (1, 2, 2, 4, 1, 2)
PLACE = (0, 1, 3, 5, 9, 10)
WIDTH = (128, 128, 256, 512, 128, 256)
GROUPS = ((3, 5), (2, 1, 0, 4))


def synthesis_table(bins):
    points, hop = 2 * bins, bins
    bin_at = np.concatenate([np.arange(0, bins, 2), np.arange(1, bins, 2)])
    angle = (bin_at[:, None] * np.arange(hop)[None, :] % points) * (2.0 * np.pi / points)
    scale = 2.0 * points**-0.5
    half = bins // 2
    parts = []
    for at in (slice(0, half), slice(half, bins)):
        parts += [np.cos(angle[at]) * scale, -np.sin(angle[at]) * scale]
    return np.concatenate(parts, axis=0).astype(np.float32).astype(ml_dtypes.bfloat16)


def hann_halves(bins):
    points = 2 * bins
    window = 0.5 - 0.5 * np.cos(np.arange(points) * (2.0 * np.pi / points))
    return window.reshape(2, bins).astype(np.float32)


def iota2(rows, cols):
    return (
        lax.broadcasted_iota(jnp.int32, (rows, cols), 0),
        lax.broadcasted_iota(jnp.int32, (rows, cols), 1),
    )


def as_bf16(mask, value=1.0):
    return jnp.where(mask, value, 0.0).astype(F32).astype(BF16)


def coarser(row, main):
    return row // 2 + jnp.where(row >= main + TILE // 2, TILE // 2, 0)


def dot(a, b):
    return jnp.dot(a, b, preferred_element_type=F32)


def dot_nt(a, b):
    return lax.dot_general(a, b, (((1,), (1,)), ((), ())), preferred_element_type=F32)


def kernel(
    n_tm,
    n_mel,
    act_one,
    act_two,
    act_three,
    act_four,
    target_one,
    target_two,
    filters,
    table,
    kernel_one,
    kernel_two,
    kernel_three,
    kernel_four,
    mel_power,
    loudness,
    spec_real,
    spec_imag,
    window,
    out,
    e1,
    e2,
    e3,
    e4,
    t1,
    t2,
    filters_v,
    table_v,
    pack_out,
    pack_in,
    corner_out,
    corner_in,
    ga,
    gb,
    gc,
    gd,
    pre,
    gain,
    filters_b,
    k2_v,
    k3_v,
    k4_v,
    power_v,
    real_v,
    imag_v,
    w4,
    w3,
    w2,
    band,
    wb,
    spec_out,
    spec_in,
    mel_out,
    mel_in,
    load_sem,
    halo_send,
    halo_recv,
    spec_send,
    spec_recv,
    mel_send,
    mel_recv,
):
    tm, mel = lax.axis_index("tm"), lax.axis_index("mel")
    length = act_one.shape[1]
    inputs = (act_one, act_two, act_three, act_four, target_one, target_two)
    wide = (e1, e2, e3, e4, t1, t2)
    frames, coarse = act_one.shape[0], act_three.shape[0]
    fine_rows, coarse_rows = e1.shape[0], e3.shape[0]
    tiles = e1.shape[1] // LANES
    share = frames // n_mel

    loads = []
    for at, (src, dst) in enumerate(zip(inputs, wide)):
        rows, cols = src.shape
        loads.append(
            pltpu.make_async_copy(
                src, dst.at[pl.ds(0, rows), pl.ds(EDGE, cols)], load_sem.at[at]
            )
        )
    for src, dst in (
        (kernel_two, k2_v),
        (kernel_three, k3_v),
        (kernel_four, k4_v),
        (mel_power, power_v),
        (spec_real, real_v),
        (spec_imag, imag_v),
        (filters.at[:, pl.ds(0, LANES)], filters_v.at[0]),
        (filters.at[:, pl.ds(LANES, LANES)], filters_v.at[1]),
        (table, table_v),
    ):
        loads.append(pltpu.make_async_copy(src, dst, load_sem.at[len(loads)]))
    for load in loads:
        load.start()

    for src, dst in zip(inputs, wide):
        rows, cols = src.shape
        dst[pl.ds(0, rows), pl.ds(0, EDGE)] = jnp.zeros((rows, EDGE), BF16)
        dst[pl.ds(0, rows), pl.ds(EDGE + cols, EDGE)] = jnp.zeros((rows, EDGE), BF16)
    pack_in[...] = jnp.zeros(pack_in.shape, BF16)
    corner_in[...] = jnp.zeros(corner_in.shape, BF16)
    spec_in[...] = jnp.zeros(spec_in.shape, BF16)
    mel_in[...] = jnp.zeros(mel_in.shape, BF16)

    barrier = pltpu.get_barrier_semaphore()

    def has(dt, dm):
        cond = jnp.bool_(True)
        if dt:
            cond = (tm > 0) if dt < 0 else (tm < n_tm - 1)
        if dm:
            side = (mel > 0) if dm < 0 else (mel < n_mel - 1)
            cond = side if not dt else jnp.logical_and(cond, side)
        return cond

    for dt in (-1, 0, 1):
        for k in range(n_mel):
            if dt == 0 and k == 0:
                continue

            def greet(dt=dt, k=k):
                pl.semaphore_signal(
                    barrier,
                    inc=1,
                    device_id={"tm": tm + dt, "mel": lax.rem(mel + k, n_mel)},
                    device_id_type=MESH,
                )

            if dt:
                pl.when(has(dt, 0))(greet)
            else:
                greet()

    halo = []

    def add_halo(dt, dm, src, dst):
        at = len(halo)
        copy = pltpu.make_async_remote_copy(
            src_ref=src,
            dst_ref=dst,
            send_sem=halo_send.at[at],
            recv_sem=halo_recv.at[at],
            device_id={"tm": tm + dt, "mel": mel + dm},
            device_id_type=MESH,
        )
        halo.append((dt, dm, copy))
        pl.when(has(dt, dm))(copy.start)

    def exchange(src, dst, send, recv):
        copies = []
        for k in range(n_mel):
            j = lax.rem(mel + k, n_mel)
            main = pl.ds(pl.multiple_of(j * share, TILE), share)
            before = pl.ds(
                pl.multiple_of(lax.rem(j * share + frames - TILE, frames), TILE), TILE
            )
            if k:
                copy = pltpu.make_async_remote_copy(
                    src_ref=src.at[main],
                    dst_ref=dst.at[mel, pl.ds(0, share)],
                    send_sem=send.at[k],
                    recv_sem=recv.at[k],
                    device_id={"tm": tm, "mel": j},
                    device_id_type=MESH,
                )
                copy.start()
                copies.append((copy, None, None))
            copy = pltpu.make_async_remote_copy(
                src_ref=src.at[before],
                dst_ref=dst.at[mel, pl.ds(share, TILE)],
                send_sem=send.at[n_mel + k],
                recv_sem=recv.at[n_mel + k],
                device_id={"tm": tm + jnp.where(j == 0, 1, 0), "mel": j},
                device_id_type=MESH,
            )
            if k:
                sends = jnp.logical_or(j > 0, tm < n_tm - 1)
                receives = jnp.logical_or(mel > 0, tm > 0)
            else:
                sends = jnp.logical_and(mel == 0, tm < n_tm - 1)
                receives = jnp.logical_and(mel == 0, tm > 0)
            pl.when(sends)(copy.start)
            copies.append((copy, sends, receives))
        dst[mel, pl.ds(0, share)] = src[pl.ds(pl.multiple_of(mel * share, TILE), share)]

        @pl.when(mel > 0)
        def _():
            dst[mel, pl.ds(share, TILE)] = src[
                pl.ds(pl.multiple_of(mel * share - TILE, TILE), TILE)
            ]

        return copies

    def finish(copies):
        for copy, sends, receives in copies:
            if sends is None:
                copy.wait_recv()
            else:
                pl.when(receives)(copy.wait_recv)
        for copy, sends, receives in copies:
            if sends is None:
                copy.wait_send()
            else:
                pl.when(sends)(copy.wait_send)

    for load in loads[:6]:
        load.wait()
    o, c = iota2(TILE, 6 * TILE)
    first_rows = jnp.zeros((TILE, 6 * TILE), jnp.bool_)
    last_rows = jnp.zeros((TILE, 6 * TILE), jnp.bool_)
    for x in range(6):
        inside = (o >= PLACE[x]) & (o < PLACE[x] + DEPTH[x])
        first_rows |= inside & (c - x * TILE == o - PLACE[x])
        last_rows |= inside & (c - x * TILE - (TILE - DEPTH[x]) == o - PLACE[x])
    picks = (as_bf16(first_rows), as_bf16(last_rows))
    counts = [src.shape[1] // EDGE for src in inputs]

    def tail_parts(x, end, chunks):
        src, dst = inputs[x], wide[x]
        row = src.shape[0] - TILE if end else 0
        return [dst[pl.ds(row, TILE), pl.ds(EDGE + at * EDGE, EDGE)] for at in chunks]

    def travels(group, end, o, k):
        found = jnp.zeros(o.shape, jnp.bool_)
        first = base = 0
        for x in group:
            inner = k - first
            row = inner % TILE - (TILE - DEPTH[x] if end else 0)
            found |= (
                (inner >= 0)
                & (inner < counts[x] * TILE)
                & (row >= 0)
                & (row < DEPTH[x])
                & (o == base + DEPTH[x] * (inner // TILE) + row)
            )
            first += counts[x] * TILE
            base += counts[x] * DEPTH[x]
        return found

    pack_rows = pack_out.shape[2]
    for g, group in enumerate(GROUPS):
        o, k = iota2(pack_rows, sum(counts[x] for x in group) * TILE)
        for end in (0, 1):
            parts = [p for x in group for p in tail_parts(x, end, range(counts[x]))]
            pack_out[g, end] = dot(
                as_bf16(travels(group, end, o, k)), jnp.concatenate(parts, axis=0)
            ).astype(BF16)
    for end in (0, 1):
        for side in (0, 1):
            parts = [
                p for x in range(6) for p in tail_parts(x, end, [counts[x] - 1 if side else 0])
            ]
            corner_out[end, side] = dot(picks[end], jnp.concatenate(parts, axis=0)).astype(BF16)
    for load in loads[10:12]:
        load.wait()
    per = spec_real.shape[1]
    k, c = iota2(per, per)
    even_first = as_bf16(k == jnp.where(c < per // 2, 2 * c, 2 * c - per + 1))
    spec_out[:, pl.ds(0, per)] = dot(real_v[...].astype(BF16), even_first).astype(BF16)
    spec_out[:, pl.ds(per, per)] = dot(imag_v[...].astype(BF16), even_first).astype(BF16)

    rows_of_peers = 1 + jnp.where(tm > 0, 1, 0) + jnp.where(tm < n_tm - 1, 1, 0)
    pl.semaphore_wait(barrier, n_mel * rows_of_peers - 1)
    ends = ((1, 1), (0, -1))

    def lateral(x):
        src, dst, width = inputs[x], wide[x], WIDTH[x]
        rows, cols = src.shape
        add_halo(
            0,
            1,
            src.at[:, pl.ds(cols - width, width)],
            dst.at[pl.ds(0, rows), pl.ds(EDGE - width, width)],
        )
        add_halo(
            0,
            -1,
            src.at[:, pl.ds(0, width)],
            dst.at[pl.ds(0, rows), pl.ds(EDGE + cols, width)],
        )

    for end, dt in ends:
        add_halo(dt, 0, pack_out.at[0, end], pack_in.at[0, 1 - end])
    for x in GROUPS[0]:
        lateral(x)
    for end, dt in ends:
        add_halo(dt, 1, corner_out.at[end, 1], corner_in.at[1 - end, 0])
        add_halo(dt, -1, corner_out.at[end, 0], corner_in.at[1 - end, 1])
    needed_first = len(halo)
    for end, dt in ends:
        add_halo(dt, 0, pack_out.at[1, end], pack_in.at[1, 1 - end])
    for x in GROUPS[1]:
        lateral(x)
    spec_copies = exchange(spec_out, spec_in, spec_send, spec_recv)

    for load in loads[6:10]:
        load.wait()
    w4[...] = jnp.zeros(w4.shape, BF16)
    w3[...] = jnp.zeros(w3.shape, BF16)
    half = LANES // 2
    blank = jnp.zeros((half, half), F32)
    for i in range(3):
        for k in range(4):
            lanes = pl.ds((i * 4 + k) * LANES, LANES)
            for n in range(2):
                j = n - (k - 1)
                if abs(j) <= 1:
                    w4[pl.ds(n * LANES, LANES), lanes] = k4_v[i, j + 1]
                    w3[pl.ds(n * LANES, half), lanes] = k3_v[i, j + 1]
                    w3[pl.ds(n * LANES + half, half), lanes] = k3_v[i, j + 1]
                for a in range(2):
                    pair = []
                    for b in range(2):
                        j = (2 * n + a) - (2 * (k - 1) + b)
                        pair.append(
                            k2_v[i, j + 1].astype(F32) if abs(j) <= 1 else blank
                        )
                    w2[pl.ds(n * LANES + a * half, half), lanes] = jnp.concatenate(
                        pair, axis=1
                    ).astype(BF16)
    mels = mel_power.shape[0]
    one = kernel_one[...].astype(F32)
    one = jnp.concatenate([one, one], axis=2)
    reach = 2 * (tiles - SIDE)
    row, lane = iota2(band.shape[1], LANES)
    d = row - reach - lane // half
    for i in range(3):
        value = jnp.zeros(d.shape, F32)
        for j in range(3):
            value = jnp.where(d == j - 1, one[i, j][None, :], value)
        band[i] = value
    for s in range(2, tiles - 2):
        for i in range(3):
            at = reach - 2 * (s - SIDE)
            wb[s, pl.ds(i * mels, mels)] = band[i, pl.ds(at, mels)].astype(BF16)
        wb[s, pl.ds(3 * mels, mels)] = jnp.zeros((mels, LANES), BF16)
    for g in (gb, gc):
        for s in (1, tiles - 2):
            for i in range(3):
                g[i, s] = jnp.zeros(g.shape[2:], BF16)

    loud = loudness[...]
    level = loud / (1.0 + loud * jnp.transpose(power_v[...]))
    level = jnp.concatenate([level, level], axis=1)
    lane = lax.broadcasted_iota(jnp.int32, level.shape, 1)
    gain[...] = jnp.where(lane // mels == lax.rem(mel, 2), level, 0.0)

    def tile_at(s, count=1):
        return pl.ds(pl.multiple_of(s * LANES, LANES), count * LANES)

    def prepare(s, pairs, fine_at, coarse_at, matrix):
        rows_at = pl.ds(coarse_at, matrix.shape[0])
        x = e2[pl.ds(fine_at, matrix.shape[1]), tile_at(s, 2 * pairs)]
        sums = dot(matrix, jnp.maximum(x, jnp.zeros_like(x)))
        low = lax.broadcasted_iota(jnp.int32, (matrix.shape[0], LANES), 1) < half
        for u in range(pairs):
            want = t1[rows_at, tile_at((s - SIDE) // 2 + SIDE + u)].astype(F32)
            turned = pltpu.roll(want, half, 1)
            wants = (jnp.where(low, want, turned), jnp.where(low, turned, want))
            for n in range(2):
                at = 2 * u + n
                block = sums[:, at * LANES : (at + 1) * LANES]
                pre[s + at, rows_at] = 0.25 * (block + pltpu.roll(block, half, 1) - wants[n])

    r, s_ = iota2(coarse, frames)
    pool_main = as_bf16(s_ // 2 == r, 0.25)
    r, s_ = iota2(TILE, TILE)
    pool_tail = as_bf16(coarser(s_, 0) == r, 0.25)

    def early(q, carry):
        prepare(SIDE + 8 * q, 4, 0, 0, pool_main)
        return carry

    for q in range((tiles - 2 * SIDE) // 8):
        early(q, 0)

    def arrive(g):
        for dt, dm, copy in halo[needed_first:] if g else halo[:needed_first]:
            pl.when(has(-dt, -dm))(copy.wait_recv)
        group = GROUPS[g]
        k, o = iota2(sum(counts[x] for x in group) * TILE, pack_rows)
        spots = jnp.concatenate(
            [as_bf16(travels(group, 1, o, k)), as_bf16(travels(group, 0, o, k))], axis=1
        )
        both = jnp.concatenate([pack_in[g, 0], pack_in[g, 1]], axis=0)
        placed = dot(spots, both).astype(BF16)
        first = 0
        for x in group:
            for at in range(counts[x]):
                wide[x][pl.ds(inputs[x].shape[0], TILE), pl.ds(EDGE + at * EDGE, EDGE)] = placed[
                    first : first + TILE
                ]
                first += TILE

    arrive(0)
    o, c = iota2(6 * TILE, 2 * TILE)
    spots = jnp.zeros((6 * TILE, 2 * TILE), jnp.bool_)
    for x in range(6):
        for at, base in ((0, TILE - DEPTH[x]), (1, 0)):
            r, p = o - x * TILE - base, c - at * TILE - PLACE[x]
            spots |= (r == p) & (r >= 0) & (r < DEPTH[x])
    spots = as_bf16(spots)
    for side in (0, 1):
        both = jnp.concatenate([corner_in[0, side], corner_in[1, side]], axis=0)
        placed = dot(spots, both).astype(BF16)
        for x, (src, dst) in enumerate(zip(inputs, wide)):
            at = pl.ds((counts[x] + 1) * EDGE if side else 0, EDGE)
            dst[pl.ds(src.shape[0], TILE), at] = placed[x * TILE : (x + 1) * TILE]

    def shifted(g, s, value):
        rows = value.shape[0]
        g[0, s] = pltpu.roll(value, rows - 1, 0).astype(BF16)
        g[1, s] = value.astype(BF16)
        g[2, s] = pltpu.roll(value, 1, 0).astype(BF16)

    r, s_ = iota2(coarse_rows, coarse_rows)
    mean_rows = as_bf16(r // 2 == s_ // 2, 0.25)
    r, s_ = iota2(coarse_rows, t2.shape[0])
    spread_two = as_bf16(coarser(r, coarse) == s_)

    batch = 4

    def top(b, carry):
        x = e4[:, tile_at(2 * batch * b, 2 * batch)]
        means = dot(mean_rows, jnp.maximum(x, jnp.zeros_like(x)))
        wanted = dot(spread_two, t2[:, tile_at(batch * b + SIDE // 2, batch)])
        for u in range(batch):
            one_, two = (means[:, (2 * u + n) * LANES : (2 * u + n + 1) * LANES] for n in (0, 1))
            diff = 0.25 * (one_ + two - wanted[:, u * LANES : (u + 1) * LANES])
            for n in range(2):
                at = 2 * u + n
                mask = x[:, at * LANES : (at + 1) * LANES].astype(F32) > 0
                shifted(ga, 2 * batch * b + at, jnp.where(mask, diff, 0.0))
        return carry

    for b in range(tiles // (2 * batch)):
        top(b, 0)

    arrive(1)
    for s in (2, tiles - 4):
        prepare(s, 1, 0, 0, pool_main)
    prepare(2, (tiles - 4) // 2, frames, coarse, pool_tail)

    def conv(g, weights, group, epilogue):
        rows = g.shape[2]
        pairs = (tiles - 4) // 2

        def step(q, carry):
            base = 2 + 2 * group * q
            lhs = jnp.concatenate(
                [
                    jnp.concatenate(
                        [g[i, base + 2 * u - 1 + k] for i in range(3) for k in range(4)], axis=1
                    )
                    for u in range(group)
                ],
                axis=0,
            )
            result = dot_nt(lhs, weights[...])
            for u in range(group):
                epilogue(base + 2 * u, result[u * rows : (u + 1) * rows])
            return carry

        for q in range(pairs // group):
            step(q, 0)

    def third(s, value):
        x = e3[:, tile_at(s, 2)].astype(F32)
        masked = jnp.where(x > 0, value, 0.0)
        for n in range(2):
            shifted(gb, s + n, masked[:, n * LANES : (n + 1) * LANES])

    conv(ga, w4, 6, third)

    r, s_ = iota2(fine_rows, coarse_rows)
    spread_rows = as_bf16(coarser(r, frames) == s_)

    def second(s, value):
        x = e2[:, tile_at(s, 2)].astype(F32)
        parts = []
        for n in range(2):
            lanes = slice(n * LANES, (n + 1) * LANES)
            parts.append((0.25 * value[:, lanes] + pre[s + n]).astype(BF16))
        fine = dot(spread_rows, jnp.concatenate(parts, axis=1))
        masked = jnp.where(x > 0, fine, 0.0)
        for n in range(2):
            shifted(gc, s + n, masked[:, n * LANES : (n + 1) * LANES])

    conv(gb, w3, 6, second)

    def first(s, value):
        x = e1[:, tile_at(s, 2)].astype(F32)
        masked = jnp.where(x > 0, value, 0.0).astype(BF16)
        for n in range(2):
            gd[s + n] = masked[:, n * LANES : (n + 1) * LANES]

    conv(gc, w2, 6, first)

    total = jnp.zeros((fine_rows, 4 * mels), F32)
    span = 12
    for s in range(2, tiles - 2, span):
        total += dot_nt(
            jnp.concatenate([gd[s + k] for k in range(span)], axis=1),
            jnp.concatenate([wb[s + k] for k in range(span)], axis=1),
        )
    left, right = total[:, : 2 * mels], total[:, 2 * mels :]
    grad_log = (
        pltpu.roll(left, fine_rows - 1, 0) + pltpu.roll(left, mels, 1) + pltpu.roll(right, 1, 0)
    )[:frames, :mels]
    mel_out[...] = (jnp.concatenate([grad_log, grad_log], axis=1) * gain[...]).astype(BF16)
    mel_copies = exchange(mel_out, mel_in, mel_send, mel_recv)

    for dt, dm, copy in halo:
        pl.when(has(dt, dm))(copy.wait_send)
    loads[12].wait()
    loads[13].wait()
    bins = filters.shape[0]
    for a in range(2):
        for odd in (0, 1):
            filters_b[pl.ds(odd * (bins // 2), bins // 2), pl.ds(a * LANES, LANES)] = filters_v[
                a, pl.ds(odd, bins // 2, stride=2), :
            ].astype(BF16)
    finish(spec_copies)
    low = lax.broadcasted_iota(jnp.int32, (spec_in.shape[1], per), 1) < per // 2
    specs = ([], [])
    for part in range(2):
        for a in range(n_mel // 2):
            one_, two = (
                spec_in[2 * a + b, :, pl.ds(part * per, per)].astype(F32) for b in (0, 1)
            )
            specs[0].append(jnp.where(low, one_, pltpu.roll(two, per // 2, 1)))
            specs[1].append(jnp.where(low, pltpu.roll(one_, per // 2, 1), two))
    specs = [jnp.concatenate(parts, axis=1) for parts in specs]
    loads[14].wait()
    finish(mel_copies)

    whole = jnp.concatenate(
        [mel_in[2 * a] + mel_in[2 * a + 1] for a in range(n_mel // 2)], axis=1
    )
    power = dot_nt(whole, filters_b[...])
    made = []
    for odd in (0, 1):
        level = power[:, odd * (bins // 2) : (odd + 1) * (bins // 2)]
        grads = (jnp.concatenate([level, level], axis=1) * specs[odd]).astype(BF16)
        made.append(dot(grads, table_v[pl.ds(odd * bins, bins), :]))
    hop = made[0].shape[1]
    halves = window[...]
    blocks = (made[0] + made[1]) * halves[0:1] + pltpu.roll(
        (made[0] - made[1]) * halves[1:2], 1, 0
    )
    for a in range(hop // LANES):
        out[pl.ds(a, share, stride=hop // LANES), :] = blocks[
            :share, a * LANES : (a + 1) * LANES
        ]


def shards(
    act_one,
    act_two,
    act_three,
    act_four,
    target_one,
    target_two,
    kernel_one,
    kernel_two,
    kernel_three,
    kernel_four,
    mel_power,
    loudness,
    filters,
    spec_real,
    spec_imag,
):
    n_tm, n_mel = lax.axis_size("tm"), lax.axis_size("mel")
    frames, mels = mel_power.shape
    bins = filters.shape[0]
    table = jnp.asarray(synthesis_table(bins))
    share = frames // n_mel
    ext = lambda a: pltpu.VMEM((a.shape[0] + TILE, a.shape[1] + 2 * EDGE), BF16)
    length = act_one.shape[1]
    tiles = (length + 2 * EDGE) // LANES
    fine_rows, coarse_rows = frames + TILE, frames // 2 + TILE
    arrays = (act_one, act_two, act_three, act_four, target_one, target_two)
    pack_rows = max(
        sum(DEPTH[x] * (arrays[x].shape[1] // EDGE) for x in group) for group in GROUPS
    )
    pack_rows = -(-pack_rows // TILE) * TILE
    any_spec = pl.BlockSpec(memory_space=pl.ANY)
    vmem = pl.BlockSpec(memory_space=pltpu.VMEM)
    result = pl.pallas_call(
        functools.partial(kernel, n_tm, n_mel),
        out_shape=jax.ShapeDtypeStruct((share * bins // LANES, LANES), F32),
        in_specs=[any_spec] * 8 + [vmem] + [any_spec] * 4 + [vmem] + [any_spec] * 2 + [vmem],
        out_specs=vmem,
        scratch_shapes=[
            ext(act_one),
            ext(act_two),
            ext(act_three),
            ext(act_four),
            ext(target_one),
            ext(target_two),
            pltpu.VMEM((2, bins, LANES), F32),
            pltpu.VMEM(table.shape, BF16),
            pltpu.VMEM((2, 2, pack_rows, EDGE), BF16),
            pltpu.VMEM((2, 2, pack_rows, EDGE), BF16),
            pltpu.VMEM((2, 2, TILE, EDGE), BF16),
            pltpu.VMEM((2, 2, TILE, EDGE), BF16),
            pltpu.VMEM((3, tiles, coarse_rows, LANES), BF16),
            pltpu.VMEM((3, tiles, coarse_rows, LANES), BF16),
            pltpu.VMEM((3, tiles, fine_rows, LANES), BF16),
            pltpu.VMEM((tiles, fine_rows, LANES), BF16),
            pltpu.VMEM((tiles, coarse_rows, LANES), F32),
            pltpu.VMEM((frames, 2 * mels), F32),
            pltpu.VMEM(filters.shape, BF16),
            pltpu.VMEM(kernel_two.shape, BF16),
            pltpu.VMEM(kernel_three.shape, BF16),
            pltpu.VMEM(kernel_four.shape, BF16),
            pltpu.VMEM((mels, frames), F32),
            pltpu.VMEM(spec_real.shape, F32),
            pltpu.VMEM(spec_imag.shape, F32),
            pltpu.VMEM((2 * LANES, 12 * LANES), BF16),
            pltpu.VMEM((2 * LANES, 12 * LANES), BF16),
            pltpu.VMEM((2 * LANES, 12 * LANES), BF16),
            pltpu.VMEM((3, 2 * (tiles + SIDE) + mels, LANES), F32),
            pltpu.VMEM((tiles, 4 * mels, LANES), BF16),
            pltpu.VMEM((frames, 2 * spec_real.shape[1]), BF16),
            pltpu.VMEM((n_mel, share + TILE, 2 * spec_real.shape[1]), BF16),
            pltpu.VMEM((frames, 2 * mels), BF16),
            pltpu.VMEM((n_mel, share + TILE, 2 * mels), BF16),
            pltpu.SemaphoreType.DMA((15,)),
            pltpu.SemaphoreType.DMA((20,)),
            pltpu.SemaphoreType.DMA((20,)),
            pltpu.SemaphoreType.DMA((2 * n_mel,)),
            pltpu.SemaphoreType.DMA((2 * n_mel,)),
            pltpu.SemaphoreType.DMA((2 * n_mel,)),
            pltpu.SemaphoreType.DMA((2 * n_mel,)),
        ],
        compiler_params=pltpu.CompilerParams(
            collective_id=0, has_side_effects=True, vmem_limit_bytes=56 * 2**20
        ),
        name="wave_gradient",
    )(
        act_one,
        act_two,
        act_three,
        act_four,
        target_one,
        target_two,
        filters,
        table,
        jnp.transpose(kernel_one, (0, 2, 1, 3)).reshape(3, 3, kernel_one.shape[3]),
        kernel_two,
        kernel_three,
        kernel_four,
        mel_power.T,
        loudness.reshape(1, mels),
        spec_real,
        spec_imag,
        jnp.asarray(hann_halves(bins)),
    )
    return result.reshape(-1)


def solution(mesh):
    return jax.shard_map(
        shards,
        mesh=mesh,
        in_specs=(
            P("tm", "mel"),
            P("tm", "mel"),
            P("tm", "mel"),
            P("tm", "mel"),
            P("tm", "mel"),
            P("tm", "mel"),
            P(),
            P(),
            P(),
            P(),
            P("tm", "mel"),
            P("mel"),
            P(),
            P("tm", "mel"),
            P("tm", "mel"),
        ),
        out_specs=P(("tm", "mel")),
        check_vma=False,
    )
```
